32 devices in a mesh: dp: 2 (over x), expert: 16 (over z, y, core).
Axes of the slice: x: 2, y: 2, z: 4, core: 2. Of those that a mesh axis runs over, the one named last changes fastest.
Arguments:
- tokens: bfloat16 [4096, 2048], P(('dp', 'expert')), may hold values from -6 to 6
- out_grad: bfloat16 [4096, 2048], P(('dp', 'expert')), may hold values from -3 to 3
- expert_ids: int32 [4096, 1], P(('dp', 'expert')), may hold values from 0 to 15, as said below
- gates: float32 [4096, 1], P(('dp', 'expert')), may hold values from 0.1 to 1
- w_gate: bfloat16 [16, 2048, 384], P('expert', 'dp'), may hold values from -0.125 to 0.125
- w_up: bfloat16 [16, 2048, 384], P('expert', 'dp'), may hold values from -0.125 to 0.125
- w_down: bfloat16 [16, 384, 2048], P('expert', None, 'dp'), may hold values from -0.3125 to 0.3125
Outputs:
- input_grad: bfloat16 [4096, 2048], P(('dp', 'expert'))
- gate_grad: bfloat16 [16, 2048, 384], P('expert', 'dp')
- up_grad: bfloat16 [16, 2048, 384], P('expert', 'dp')
- down_grad: bfloat16 [16, 384, 2048], P('expert')
The draws below stay inside these ranges and needn't reach their ends.
Inputs may be any that keep to these rules, and one draw needn't show every extreme that they name: `expert_ids`: among the rows of one device no expert is named more than 24 times; 1 expert, the same ones for every device, are named exactly 24 times by every device.
All inputs are finite; a program needn't handle non-finite values.
Results may differ from the reference program's by a relative error of at most 0.013.
Values may be sent and summed in bfloat16 or wider, within the bound.
No kernel may reach another device: no remote copies, remote signals or barrier semaphores. Data moves between devices by JAX's collectives and lax.ppermute only.
A program may use at most 64 MiB of HBM per device.

```python
import jax
import jax.numpy as jnp
from jax import lax

D = 2048
HID = 384
TOK_DEV = 128
TOPK = 1
EXPERTS = 16
MOST = 24
HOT = 1
CAP = 384
GROUP_TOKENS = 2048
TOKENS = 4096
N_DP = 2


def draw_expert_ids(key, part):
    blocks = TOKENS // TOK_DEV
    entries = TOK_DEV * TOPK
    cold_count = EXPERTS - HOT
    cold_rows = entries - HOT * MOST
    sorting = jax.random.permutation(jax.random.fold_in(key, 11), EXPERTS).astype(jnp.int32)

    def one_block(block_index):
        block_key = jax.random.fold_in(jax.random.fold_in(key, 23), block_index)
        weights = jax.random.randint(jax.random.fold_in(block_key, 1), (cold_count,), 2, 7).astype(jnp.int32)
        quotas = cold_rows * weights // jnp.sum(weights)
        leftover = cold_rows - jnp.sum(quotas)
        quotas = quotas + (jnp.arange(cold_count, dtype=jnp.int32) < leftover).astype(jnp.int32)
        counts = jnp.zeros((EXPERTS,), jnp.int32).at[sorting[HOT:]].set(quotas)
        counts = counts.at[sorting[:HOT]].set(MOST)
        labels = jnp.repeat(jnp.arange(EXPERTS, dtype=jnp.int32), counts, total_repeat_length=entries)
        id_table = labels.reshape(TOPK, TOK_DEV).T
        shuffle = jax.random.permutation(jax.random.fold_in(block_key, 2), TOK_DEV)
        return id_table[shuffle]
    every_block = jax.vmap(one_block)(jnp.arange(blocks, dtype=jnp.int32))
    return every_block.reshape(TOKENS, TOPK).astype(jnp.int32)


def level_of(stream_key, shape, split, low, top_value):
    gain, own = 1.0, jax.random.fold_in(stream_key, 6)
    for axis_at, blocks in split:
        steps = jnp.exp(jax.random.uniform(jax.random.fold_in(own, axis_at), (blocks,), jnp.float32, low / len(split), top_value / len(split)))
        gain = gain * jnp.repeat(steps, shape[axis_at] // blocks).reshape([-1 if axis == axis_at else 1 for axis in range(len(shape))])
    return gain


def noise(rng, extent, deviation, limit, shards=(), kind=jnp.bfloat16):
    gain = level_of(rng, extent, shards, -0.22, 0.18) if shards else 1.0
    drawn = jax.random.normal(rng, extent, jnp.float32) * deviation * gain
    return jnp.minimum(jnp.maximum(drawn, -limit), limit).astype(kind)


def setup_inputs(seed: int = 0) -> dict:
    splits = jax.random.split(jax.random.key(seed), 8)
    return {
        "tokens": noise(splits[0], (TOKENS, D), 1.0, 6.0, ((0, 32),)),
        "out_grad": noise(splits[1], (TOKENS, D), 0.5, 3.0, ((0, 32),)),
        "expert_ids": draw_expert_ids(jax.random.fold_in(splits[7], 71), 0),
        "gates": jnp.clip(0.1 + 0.9 * jax.random.uniform(splits[3], (TOKENS, TOPK), jnp.float32) ** level_of(splits[3], (TOKENS, TOPK), ((0, 32),), -0.2, 0.2), 0.1, 1.0),
        "w_gate": noise(splits[4], (EXPERTS, D, HID), D ** -0.5, 0.125, ((0, 16), (1, 2))),
        "w_up": noise(splits[5], (EXPERTS, D, HID), D ** -0.5, 0.125, ((0, 16), (1, 2))),
        "w_down": noise(splits[6], (EXPERTS, HID, D), HID ** -0.5, 0.3125, ((0, 16), (2, 2))),
    }


def reference(tokens, out_grad, expert_ids, gates, w_gate, w_up, w_down):
    group_entries = GROUP_TOKENS * TOPK
    grouped = expert_ids.reshape(N_DP, group_entries)
    sorting = jnp.argsort(grouped, axis=1, stable=True).astype(jnp.int32)
    expert_range = jnp.arange(EXPERTS, dtype=jnp.int32)
    counts = jnp.sum((grouped[:, :, None] == expert_range[None, None, :]).astype(jnp.int32), axis=1).astype(jnp.int32)
    starts = (jnp.cumsum(counts, axis=1) - counts).astype(jnp.int32)
    slot_lane = jnp.arange(CAP, dtype=jnp.int32)
    group_base = (jnp.arange(N_DP, dtype=jnp.int32) * group_entries)[:, None]
    flat_gates = gates.reshape(-1)

    def per_expert(accumulated, expert):
        gate_w = w_gate[expert]
        up_w = w_up[expert]
        down_w = w_down[expert]
        joined = jnp.concatenate([gate_w, up_w], axis=1)
        positions = jnp.minimum(starts[:, expert][:, None] + slot_lane[None, :], group_entries - 1).astype(jnp.int32)
        usable = (slot_lane[None, :] < counts[:, expert][:, None]).reshape(-1)
        entry_ids = (jnp.take_along_axis(sorting, positions, axis=1) + group_base).reshape(-1).astype(jnp.int32)
        token_ids = (entry_ids // TOPK).astype(jnp.int32)
        inputs = jnp.where(usable[:, None], tokens[token_ids], jnp.zeros((), tokens.dtype))
        slot_gate = jnp.where(usable, flat_gates[entry_ids], jnp.zeros((), flat_gates.dtype))
        scaled = (slot_gate[:, None] * out_grad[token_ids].astype(jnp.float32)).astype(jnp.bfloat16)
        preact = jnp.dot(inputs, joined, preferred_element_type=jnp.float32)
        hidden_grad = lax.dot_general(scaled, down_w, (((1,), (1,)), ((), ())), preferred_element_type=jnp.float32)
        gate_pre = preact[:, :HID]
        up_pre = preact[:, HID:]
        sigmoid = jax.nn.sigmoid(gate_pre)
        silu_value = gate_pre * sigmoid
        activated = (silu_value * up_pre).astype(jnp.bfloat16)
        gate_side = (hidden_grad * up_pre * sigmoid * (1.0 + gate_pre * (1.0 - sigmoid))).astype(jnp.bfloat16)
        up_side = (hidden_grad * silu_value).astype(jnp.bfloat16)
        both_sides = jnp.concatenate([gate_side, up_side], axis=1)
        down_parts = jnp.einsum("rch,rcd->rhd", activated.reshape(N_DP, CAP, HID).astype(jnp.float32), scaled.reshape(N_DP, CAP, D).astype(jnp.float32))
        down_round = lax.optimization_barrier(down_parts.astype(jnp.bfloat16))
        down_total = jnp.sum(down_round.astype(jnp.float32), axis=0).astype(jnp.bfloat16)
        join_parts = jnp.einsum("rcd,rcj->rdj", inputs.reshape(N_DP, CAP, D).astype(jnp.float32), both_sides.reshape(N_DP, CAP, 2 * HID).astype(jnp.float32))
        join_round = lax.optimization_barrier(join_parts.astype(jnp.bfloat16))
        join_total = jnp.sum(join_round.astype(jnp.float32), axis=0).astype(jnp.bfloat16)
        slot_grad = lax.dot_general(both_sides, joined, (((1,), (1,)), ((), ())), preferred_element_type=jnp.float32)
        slot_round = lax.optimization_barrier(slot_grad.astype(jnp.bfloat16))
        adding = jnp.where(usable[:, None], slot_round.astype(jnp.float32), jnp.zeros((), jnp.float32))
        accumulated = accumulated.at[token_ids].add(adding)
        return accumulated, (join_total[:, :HID], join_total[:, HID:], down_total)

    start_grad = jnp.zeros((TOKENS, D), jnp.float32)
    summed, outputs = lax.scan(per_expert, start_grad, jnp.arange(EXPERTS, dtype=jnp.int32))
    gate_grad, up_grad, down_grad = outputs
    return summed.astype(jnp.bfloat16), gate_grad, up_grad, down_grad
```

```python
import jax
import jax.numpy as jnp
from jax import lax
from jax.sharding import PartitionSpec as P

BF16 = jnp.bfloat16
F32 = jnp.float32
BOTH = ("dp", "expert")


def dot(a, b, contract):
    return lax.dot_general(a, b, ((contract[:1], contract[1:]), ((), ())), preferred_element_type=F32)


def sum_over_dp(partial):
    n_dp = lax.axis_size("dp")
    if n_dp == 1:
        return partial
    if n_dp == 2:
        return partial + lax.ppermute(partial.astype(BF16), "dp", [(0, 1), (1, 0)]).astype(F32)
    return lax.psum(partial, "dp")


def gather_columns(half):
    n_dp = lax.axis_size("dp")
    if n_dp != 2:
        return lax.all_gather(half, "dp", axis=1, tiled=True)
    other = lax.ppermute(half, "dp", [(0, 1), (1, 0)])
    first = lax.axis_index("dp") == 0
    return jnp.concatenate([jnp.where(first, half, other), jnp.where(first, other, half)], axis=1)


def on_device(tokens, out_grad, expert_ids, gates, w_gate, w_up, w_down):
    n_dp = lax.axis_size("dp")
    experts = lax.axis_size("expert")
    tok_rows, width = tokens.shape
    per_token = expert_ids.shape[1]
    hidden = w_gate.shape[2]
    entries = tok_rows * per_token
    depth = 3 * entries // experts
    slots = experts * depth
    cols = width // n_dp
    rows = experts * depth

    flat_ids = expert_ids.reshape(entries)
    onehot = (flat_ids[:, None] == jnp.arange(experts, dtype=jnp.int32)[None, :]).astype(F32)
    earlier = (
        jnp.arange(entries, dtype=jnp.int32)[None, :] < jnp.arange(entries, dtype=jnp.int32)[:, None]
    ).astype(F32)
    before = dot(earlier, onehot, (1, 0))
    ranking = jnp.sum(before * onehot, axis=1).astype(jnp.int32)
    slot_of_entry = flat_ids * depth + ranking
    place = (jnp.arange(slots, dtype=jnp.int32)[:, None] == slot_of_entry[None, :]).astype(BF16)

    def dispatch(table):
        table = jnp.repeat(table, per_token, axis=0) if table.shape[0] != entries else table
        halves = table.reshape(entries, n_dp, cols)
        sent = jnp.stack(
            [dot(place, halves[:, part], (1, 0)).astype(BF16) for part in range(n_dp)]
        ).reshape(n_dp * experts, depth, cols)
        got = lax.all_to_all(sent, BOTH, split_axis=0, concat_axis=0, tiled=True)
        return got.reshape(n_dp * rows, cols)

    scaled = (
        (gates[:, :, None] * out_grad.astype(F32)[:, None, :]).astype(BF16).reshape(entries, width)
    )
    rows_in = dispatch(tokens)
    grads_in = dispatch(scaled)

    joined = jnp.concatenate([w_gate[0], w_up[0]], axis=1)
    preact = sum_over_dp(dot(rows_in, joined, (1, 0)))
    hidden_grad = sum_over_dp(dot(grads_in, w_down[0], (1, 1)))

    gate_pre = preact[:, :hidden]
    up_pre = preact[:, hidden:]
    sigmoid = jax.nn.sigmoid(gate_pre)
    silu_value = gate_pre * sigmoid
    activated = (silu_value * up_pre).astype(BF16)
    gate_side = (hidden_grad * up_pre * sigmoid * (1.0 + gate_pre * (1.0 - sigmoid))).astype(BF16)
    up_side = (hidden_grad * silu_value).astype(BF16)
    sides = jnp.concatenate([gate_side, up_side], axis=1)

    slot_grad = dot(sides, joined, (1, 1)).astype(BF16).reshape(n_dp * experts, depth, cols)
    returned = lax.all_to_all(slot_grad, BOTH, split_axis=0, concat_axis=0, tiled=True).reshape(
        n_dp, slots, cols
    )

    def over_groups(left, right):
        total = 0.0
        for group in range(n_dp):
            part = slice(group * rows, (group + 1) * rows)
            total = total + dot(left[part], right[part], (0, 0)).astype(BF16).astype(F32)
        return total.astype(BF16)

    down_grad = gather_columns(over_groups(activated, grads_in))[None]
    joined_grad = over_groups(rows_in, sides)

    picked = jnp.concatenate(
        [dot(place, returned[part], (0, 0)) for part in range(n_dp)], axis=1
    )
    input_grad = jnp.sum(picked.reshape(tok_rows, per_token, width), axis=1).astype(BF16)
    return (input_grad, joined_grad[:, :hidden][None], joined_grad[:, hidden:][None], down_grad)


def solution(mesh):
    rows = P(BOTH, None)
    in_specs = (
        rows,
        rows,
        rows,
        rows,
        P("expert", "dp", None),
        P("expert", "dp", None),
        P("expert", None, "dp"),
    )
    out_specs = (
        rows,
        P("expert", "dp", None),
        P("expert", "dp", None),
        P("expert", None, None),
    )
    return jax.shard_map(
        on_device, mesh=mesh, in_specs=in_specs, out_specs=out_specs, check_vma=False
    )
```

```python
import functools

import jax
import jax.numpy as jnp
from jax import lax
from jax.experimental import pallas as pl
from jax.experimental.pallas import tpu as pltpu
from jax.sharding import PartitionSpec as P

BF16 = jnp.bfloat16
F32 = jnp.float32
BOTH = ("dp", "expert")
LATE_FLOPS = 100_000_000_000


def dot(a, b, contract):
    return lax.dot_general(a, b, ((contract[:1], contract[1:]), ((), ())), preferred_element_type=F32)


def swap(x):
    return lax.ppermute(x, "dp", [(0, 1), (1, 0)])


def exchange(x, axes):
    return lax.all_to_all(x, axes, split_axis=0, concat_axis=0, tiled=True)


def place_matrix(expert_ids, experts, depth):
    entries = expert_ids.size
    flat_ids = expert_ids.reshape(entries)
    order = jnp.arange(entries, dtype=jnp.int32)
    onehot = (flat_ids[:, None] == jnp.arange(experts, dtype=jnp.int32)[None, :]).astype(BF16)
    earlier = (order[None, :] < order[:, None]).astype(BF16)
    before = dot(earlier, onehot, (1, 0))
    ranking = jnp.sum(before * onehot.astype(F32), axis=1).astype(jnp.int32)
    slot_of_entry = flat_ids * depth + ranking
    return (
        jnp.arange(experts * depth, dtype=jnp.int32)[:, None] == slot_of_entry[None, :]
    ).astype(BF16)


def sides_of(gate_pre, up_pre, hidden_grad):
    sigmoid = jax.nn.sigmoid(gate_pre)
    silu_value = gate_pre * sigmoid
    activated = (silu_value * up_pre).astype(BF16)
    gate_side = (hidden_grad * up_pre * sigmoid * (1.0 + gate_pre * (1.0 - sigmoid))).astype(BF16)
    up_side = (hidden_grad * silu_value).astype(BF16)
    return activated, jnp.concatenate([gate_side, up_side], axis=1)


def sum_parts(first, second):
    return (first.astype(BF16).astype(F32) + second.astype(BF16).astype(F32)).astype(BF16)


def scaled_rows(out_grad, gates):
    return (
        (gates[:, :, None] * out_grad.astype(F32)[:, None, :])
        .astype(BF16)
        .reshape(gates.size, out_grad.shape[1])
    )


def token_rows(tokens, per_token):
    return jnp.repeat(tokens, per_token, axis=0) if per_token > 1 else tokens


def sum_choices(picked, per_token):
    if per_token > 1:
        picked = jnp.sum(picked.reshape(-1, per_token, picked.shape[1]).astype(F32), axis=1)
    return picked.astype(BF16)


MIB = 1 << 20
IN_HBM = pl.BlockSpec(memory_space=pltpu.HBM)


def shape(*dims, dtype=BF16):
    return jax.ShapeDtypeStruct(dims, dtype)


def call(kernel, out_shapes, scratch, copies, flops, *operands):
    moved = sum(x.size * x.dtype.itemsize for x in operands)
    moved += sum(x.size * x.dtype.itemsize for x in out_shapes)
    return pl.pallas_call(
        kernel,
        out_shape=list(out_shapes),
        in_specs=[IN_HBM] * len(operands),
        out_specs=[IN_HBM] * len(out_shapes),
        scratch_shapes=[pltpu.VMEM(x.shape, x.dtype) for x in scratch]
        + [pltpu.SemaphoreType.DMA((copies,))],
        compiler_params=pltpu.CompilerParams(vmem_limit_bytes=60 * MIB),
        cost_estimate=pl.CostEstimate(flops=flops, bytes_accessed=moved, transcendentals=0),
    )(*operands)


class Mover:
    def __init__(self, semaphores):
        self.semaphores, self.count = semaphores, 0

    def start(self, source, target):
        copy = pltpu.make_async_copy(source, target, self.semaphores.at[self.count])
        self.count += 1
        copy.start()
        return copy


def wait(*copies):
    for copy in copies:
        copy.wait()


def half_at(index, half):
    return pl.ds(pl.multiple_of(index * half, half), half)


def kernel_place(
    experts, depth, ids_hbm, gates_hbm, grad_hbm, place_hbm, send_hbm, ids, gates, grad, place_at, send, sems
):
    entries = ids.shape[1]
    slots = experts * depth
    half = grad.shape[1] // 2
    move = Mover(sems)
    small = move.start(ids_hbm, ids), move.start(gates_hbm, gates)
    loads = [
        move.start(grad_hbm.at[:, pl.ds(part * half, half)], grad.at[:, pl.ds(part * half, half)])
        for part in range(2)
    ]
    wait(*small)
    onehot = (lax.broadcasted_iota(jnp.int32, (experts, entries), 0) == ids[...]).astype(F32)
    earlier = (
        lax.broadcasted_iota(jnp.int32, (entries, entries), 0)
        < lax.broadcasted_iota(jnp.int32, (entries, entries), 1)
    ).astype(BF16)
    before = dot(onehot.astype(BF16), earlier, (1, 0))
    ranking = jnp.sum(before * onehot, axis=0, keepdims=True).astype(jnp.int32)
    slot = ids[...] * depth + ranking
    place = (lax.broadcasted_iota(jnp.int32, (slots, entries), 0) == slot).astype(F32).astype(BF16)
    place_at[...] = place
    stores = [move.start(place_at, place_hbm)]
    weight = jnp.broadcast_to(gates[...], (entries, entries)).T[:, :1]
    for part in range(2):
        wait(loads[part])
        scaled = (weight * grad[:, part * half : (part + 1) * half].astype(F32)).astype(BF16)
        rows = pl.ds(part * slots, slots)
        send[rows] = dot(place, scaled, (1, 0)).astype(BF16)
        stores.append(move.start(send.at[rows], send_hbm.at[rows]))
    wait(*stores)


def kernel_core(
    rows_hbm, gate_hbm, up_hbm, other_gate_hbm, other_up_hbm, partial_hbm, remote_hbm,
    pre_hbm, act_hbm, sides_hbm, slot_hbm,
    rows, joined, partial, remote, pre_at, act, sides, slot, sems,
):
    slots, width = rows.shape
    half = width // 2
    hidden = act.shape[1]
    mine = pl.ds(pl.multiple_of(lax.axis_index("dp") * slots, slots), slots)
    move = Mover(sems)
    first = [move.start(rows_hbm.at[:, pl.ds(0, half)], rows.at[:, pl.ds(0, half)])]
    first += [
        move.start(source, joined.at[pl.ds(0, half), pl.ds(at, hidden)])
        for at, source in ((0, gate_hbm), (hidden, up_hbm))
    ]
    second = [move.start(rows_hbm.at[:, pl.ds(half, half)], rows.at[:, pl.ds(half, half)])]
    second += [
        move.start(source, joined.at[pl.ds(half, half), pl.ds(at, hidden)])
        for at, source in ((0, other_gate_hbm), (hidden, other_up_hbm))
    ]
    third = [move.start(partial_hbm.at[mine], partial), move.start(remote_hbm.at[mine], remote)]
    wait(*first)
    pre = dot(rows[:, :half], joined[:half], (1, 0))
    wait(*second)
    pre = pre + dot(rows[:, half:], joined[half:], (1, 0))
    pre_at[...] = pre.astype(BF16)
    stores = [move.start(pre_at, pre_hbm)]
    wait(*third)
    hidden_grad = partial[...] + remote[...].astype(F32)
    activated, both = sides_of(pre[:, :hidden], pre[:, hidden:], hidden_grad)
    act[...] = activated
    sides[...] = both
    stores += [move.start(act, act_hbm), move.start(sides, sides_hbm)]
    for part in range(2):
        columns = pl.ds(part * half, half)
        slot[:, part * half : (part + 1) * half] = dot(
            both, joined[part * half : (part + 1) * half], (1, 1)
        ).astype(BF16)
        stores.append(move.start(slot.at[:, columns], slot_hbm.at[:, columns]))
    wait(*stores)


def kernel_down(
    pre_hbm, partial_hbm, remote_hbm, act_hbm, grads_hbm,
    down_hbm, sides_hbm,
    pre, partial, remote, act, grads, down, sides, sems,
):
    slots, hidden = act.shape
    me = lax.axis_index("dp")
    mine = pl.ds(pl.multiple_of(me * slots, slots), slots)
    theirs = pl.ds(pl.multiple_of((1 - me) * slots, slots), slots)
    move = Mover(sems)
    first = [
        move.start(source, target)
        for source, target in (
            (pre_hbm, pre),
            (partial_hbm.at[theirs], partial),
            (remote_hbm.at[theirs], remote),
        )
    ]
    second = [
        move.start(source, target)
        for source, target in (
            (act_hbm, act),
            (grads_hbm.at[mine], grads.at[pl.ds(0, slots)]),
            (grads_hbm.at[theirs], grads.at[pl.ds(slots, slots)]),
        )
    ]
    wait(*first)
    hidden_grad = partial[...] + remote[...].astype(F32)
    act_other, sides_other = sides_of(
        pre[:, :hidden].astype(F32), pre[:, hidden:].astype(F32), hidden_grad
    )
    sides[...] = sides_other
    stores = [move.start(sides, sides_hbm)]
    wait(*second)
    down[...] = sum_parts(
        dot(act[...], grads[:slots], (0, 0)), dot(act_other, grads[slots:], (0, 0))
    )
    stores.append(move.start(down, down_hbm))
    wait(*stores)


def kernel_joined(
    rows_hbm, other_rows_hbm, sides_hbm, other_sides_hbm,
    gate_hbm, up_hbm,
    rows, other_rows, sides, other_sides, joined, sems,
):
    half = rows.shape[1]
    hidden = sides.shape[1] // 2
    move = Mover(sems)
    loads = [
        move.start(source, target)
        for source, target in (
            (rows_hbm.at[:, pl.ds(0, half)], rows),
            (sides_hbm, sides),
            (other_rows_hbm, other_rows),
            (other_sides_hbm, other_sides),
        )
    ]
    wait(*loads)
    stores = []
    for at, target in ((0, gate_hbm), (hidden, up_hbm)):
        columns = slice(at, at + hidden)
        joined[:, columns] = sum_parts(
            dot(rows[...], sides[:, columns], (0, 0)),
            dot(other_rows[...], other_sides[:, columns], (0, 0)),
        )
        stores.append(move.start(joined.at[:, pl.ds(at, hidden)], target))
    wait(*stores)


def kernel_final(
    place_hbm, returned_hbm, own_hbm, other_hbm, input_hbm, down_hbm, place, returned, out, down, sems
):
    half = out.shape[1] // 2
    me = lax.axis_index("dp")
    move = Mover(sems)
    loads = [move.start(place_hbm, place)] + [
        move.start(
            returned_hbm.at[:, pl.ds(part * half, half)], returned.at[:, pl.ds(part * half, half)]
        )
        for part in range(2)
    ]
    at = half_at(me, half), half_at(1 - me, half)
    down_loads = [
        move.start(source, down.at[part]) for part, source in enumerate((own_hbm, other_hbm))
    ]
    wait(*loads[:2])
    stores = []
    for part in range(2):
        columns = slice(part * half, (part + 1) * half)
        out[:, columns] = dot(place[...], returned[:, columns], (0, 0)).astype(BF16)
        stores.append(
            move.start(out.at[:, pl.ds(part * half, half)], input_hbm.at[:, at[part]])
        )
        wait(down_loads[part])
        stores.append(move.start(down.at[part], down_hbm.at[:, at[part]]))
        if part == 0:
            wait(loads[2])
    wait(*stores)


def on_pair(tokens, out_grad, expert_ids, gates, w_gate, w_up, w_down):
    experts = lax.axis_size("expert")
    width = tokens.shape[1]
    per_token = expert_ids.shape[1]
    hidden = w_gate.shape[2]
    entries = expert_ids.size
    depth = 3 * entries // experts
    slots = experts * depth
    half = width // 2
    first = lax.axis_index("dp") == 0

    grad_rows = token_rows(out_grad, per_token)
    place, send_grads = call(
        functools.partial(kernel_place, experts, depth),
        (shape(slots, entries), shape(2 * slots, half)),
        (
            shape(1, entries, dtype=jnp.int32),
            shape(1, entries, dtype=F32),
            shape(entries, width),
            shape(slots, entries),
            shape(2 * slots, half),
        ),
        7,
        2 * slots * entries * width,
        expert_ids.reshape(1, entries),
        gates.reshape(1, entries),
        grad_rows,
    )
    recv_grads = exchange(send_grads.reshape(2 * experts, depth, half), BOTH)
    other_gate = swap(w_gate[0])
    inputs = token_rows(tokens, per_token)
    low, high = inputs[:, :half], inputs[:, half:]
    inputs = jnp.concatenate([jnp.where(first, low, high), jnp.where(first, high, low)], axis=1)
    send_inputs = dot(place, inputs, (1, 0)).astype(BF16)
    recv_grads, other_gate, send_inputs = lax.optimization_barrier(
        (recv_grads, other_gate, send_inputs)
    )
    rows_in = exchange(send_inputs.reshape(experts, depth, width), "expert").reshape(slots, width)
    other_up = swap(w_up[0])

    grads_in = recv_grads.reshape(2 * slots, half)
    partial = dot(grads_in, w_down[0], (1, 1))
    remote = swap(partial.astype(BF16))

    other_rows = swap(rows_in[:, half:])
    pre, act, sides, slot_grad = call(
        kernel_core,
        (
            shape(slots, 2 * hidden),
            shape(slots, hidden),
            shape(slots, 2 * hidden),
            shape(slots, width),
        ),
        (
            shape(slots, width),
            shape(width, 2 * hidden),
            shape(slots, hidden, dtype=F32),
            shape(slots, hidden),
            shape(slots, 2 * hidden),
            shape(slots, hidden),
            shape(slots, 2 * hidden),
            shape(slots, width),
        ),
        13,
        8 * slots * hidden * width,
        rows_in,
        w_gate[0],
        w_up[0],
        other_gate,
        other_up,
        partial,
        remote,
    )
    other_pre = swap(pre)
    returned = exchange(slot_grad.reshape(experts, depth, width), "expert").reshape(slots, width)

    own_down, other_sides = call(
        kernel_down,
        (shape(hidden, half), shape(slots, 2 * hidden)),
        (
            shape(slots, 2 * hidden),
            shape(slots, hidden, dtype=F32),
            shape(slots, hidden),
            shape(slots, hidden),
            shape(2 * slots, half),
            shape(hidden, half),
            shape(slots, 2 * hidden),
        ),
        8,
        LATE_FLOPS,
        other_pre,
        partial,
        remote,
        act,
        grads_in,
    )
    other_down = swap(own_down)
    gate_grad, up_grad = call(
        kernel_joined,
        (shape(half, hidden), shape(half, hidden)),
        (
            shape(slots, half),
            shape(slots, half),
            shape(slots, 2 * hidden),
            shape(slots, 2 * hidden),
            shape(half, 2 * hidden),
        ),
        6,
        LATE_FLOPS,
        rows_in,
        other_rows,
        sides,
        other_sides,
    )
    picked, down_grad = call(
        kernel_final,
        (shape(entries, width), shape(hidden, width)),
        (
            shape(slots, entries),
            shape(slots, width),
            shape(entries, width),
            shape(2, hidden, half),
        ),
        9,
        2 * slots * entries * width,
        place,
        returned,
        own_down,
        other_down,
    )
    return (sum_choices(picked, per_token), gate_grad[None], up_grad[None], down_grad[None])


def on_device(tokens, out_grad, expert_ids, gates, w_gate, w_up, w_down):
    if lax.axis_size("dp") == 2:
        return on_pair(tokens, out_grad, expert_ids, gates, w_gate, w_up, w_down)
    experts = lax.axis_size("expert")
    width = tokens.shape[1]
    per_token = expert_ids.shape[1]
    hidden = w_gate.shape[2]
    depth = 3 * expert_ids.size // experts
    slots = experts * depth

    joined = lax.all_gather(
        jnp.concatenate([w_gate[0], w_up[0]], axis=1), "dp", axis=0, tiled=True
    )
    down = lax.all_gather(w_down[0], "dp", axis=1, tiled=True)
    place = place_matrix(expert_ids, experts, depth)

    def dispatch(table):
        sent = dot(place, table, (1, 0)).astype(BF16).reshape(experts, depth, width)
        return exchange(sent, "expert").reshape(slots, width)

    rows_in = dispatch(token_rows(tokens, per_token))
    grads_in = dispatch(scaled_rows(out_grad, gates))
    preact = dot(rows_in, joined, (1, 0))
    activated, sides = sides_of(
        preact[:, :hidden], preact[:, hidden:], dot(grads_in, down, (1, 1))
    )
    slot_grad = dot(sides, joined, (1, 1)).astype(BF16)
    returned = exchange(slot_grad.reshape(experts, depth, width), "expert").reshape(slots, width)
    down_grad = lax.psum(dot(activated, grads_in, (0, 0)).astype(BF16), "dp")
    joined_grad = lax.psum_scatter(
        dot(rows_in, sides, (0, 0)).astype(BF16), "dp", scatter_dimension=0, tiled=True
    )
    input_grad = sum_choices(dot(place, returned, (0, 0)), per_token)
    return (
        input_grad,
        joined_grad[:, :hidden][None],
        joined_grad[:, hidden:][None],
        down_grad[None],
    )


def solution(mesh):
    rows = P(BOTH, None)
    in_specs = (
        rows,
        rows,
        rows,
        rows,
        P("expert", "dp", None),
        P("expert", "dp", None),
        P("expert", None, "dp"),
    )
    out_specs = (
        rows,
        P("expert", "dp", None),
        P("expert", "dp", None),
        P("expert", None, None),
    )
    return jax.shard_map(
        on_device, mesh=mesh, in_specs=in_specs, out_specs=out_specs, check_vma=False
    )
```

```python
import functools

import jax
import jax.numpy as jnp
from jax import lax
from jax.experimental import pallas as pl
from jax.experimental.pallas import tpu as pltpu
from jax.sharding import PartitionSpec as P

BF16 = jnp.bfloat16
F32 = jnp.float32
BOTH = ("dp", "expert")
LATE_FLOPS = 100_000_000_000
LANES = 128


def dot(a, b, contract):
    return lax.dot_general(a, b, ((contract[:1], contract[1:]), ((), ())), preferred_element_type=F32)


def swap(x):
    return lax.ppermute(x, "dp", [(0, 1), (1, 0)])


def exchange(x, axes):
    return lax.all_to_all(x, axes, split_axis=0, concat_axis=0, tiled=True)


def place_matrix(expert_ids, experts, depth):
    entries = expert_ids.size
    flat_ids = expert_ids.reshape(entries)
    order = jnp.arange(entries, dtype=jnp.int32)
    onehot = (flat_ids[:, None] == jnp.arange(experts, dtype=jnp.int32)[None, :]).astype(BF16)
    earlier = (order[None, :] < order[:, None]).astype(BF16)
    before = dot(earlier, onehot, (1, 0))
    ranking = jnp.sum(before * onehot.astype(F32), axis=1).astype(jnp.int32)
    slot_of_entry = flat_ids * depth + ranking
    return (
        jnp.arange(experts * depth, dtype=jnp.int32)[:, None] == slot_of_entry[None, :]
    ).astype(BF16)


def sides_of(gate_pre, up_pre, hidden_grad):
    sigmoid = jax.nn.sigmoid(gate_pre)
    silu_value = gate_pre * sigmoid
    activated = (silu_value * up_pre).astype(BF16)
    gate_side = (hidden_grad * up_pre * sigmoid * (1.0 + gate_pre * (1.0 - sigmoid))).astype(BF16)
    up_side = (hidden_grad * silu_value).astype(BF16)
    return activated, jnp.concatenate([gate_side, up_side], axis=1)


def sum_parts(first, second):
    return (first.astype(BF16).astype(F32) + second.astype(BF16).astype(F32)).astype(BF16)


def scaled_rows(out_grad, gates):
    return (
        (gates[:, :, None] * out_grad.astype(F32)[:, None, :])
        .astype(BF16)
        .reshape(gates.size, out_grad.shape[1])
    )


def token_rows(tokens, per_token):
    return jnp.repeat(tokens, per_token, axis=0) if per_token > 1 else tokens


def sum_choices(picked, per_token):
    if per_token > 1:
        picked = jnp.sum(picked.reshape(-1, per_token, picked.shape[1]).astype(F32), axis=1)
    return picked.astype(BF16)


MIB = 1 << 20
IN_HBM = pl.BlockSpec(memory_space=pltpu.HBM)


def shape(*dims, dtype=BF16):
    return jax.ShapeDtypeStruct(dims, dtype)


def call(kernel, out_shapes, scratch, copies, flops, *operands):
    moved = sum(x.size * x.dtype.itemsize for x in operands)
    moved += sum(x.size * x.dtype.itemsize for x in out_shapes)
    return pl.pallas_call(
        kernel,
        out_shape=list(out_shapes),
        in_specs=[IN_HBM] * len(operands),
        out_specs=[IN_HBM] * len(out_shapes),
        scratch_shapes=[pltpu.VMEM(x.shape, x.dtype) for x in scratch]
        + [pltpu.SemaphoreType.DMA((copies,))],
        compiler_params=pltpu.CompilerParams(vmem_limit_bytes=64 * MIB),
        cost_estimate=pl.CostEstimate(flops=flops, bytes_accessed=moved, transcendentals=0),
    )(*operands)


class Mover:
    def __init__(self, semaphores):
        self.semaphores, self.count = semaphores, 0

    def start(self, source, target):
        copy = pltpu.make_async_copy(source, target, self.semaphores.at[self.count])
        self.count += 1
        copy.start()
        return copy


def wait(*copies):
    for copy in copies:
        copy.wait()


def half_at(index, half):
    return pl.ds(pl.multiple_of(index * half, half), half)


def zero_one(condition):
    return condition.astype(F32).astype(BF16)


def lane_row(count):
    return lax.broadcasted_iota(jnp.int32, (1, count), 1)


def row_index(rows, columns):
    return lax.broadcasted_iota(jnp.int32, (rows, columns), 0)


def with_mark(rows, mark):
    return jnp.concatenate([rows, jnp.broadcast_to(mark, (rows.shape[0], LANES))], axis=1).astype(BF16)


def ranks(ids, experts):
    entries = ids.shape[1]
    onehot = (row_index(experts, entries) == ids).astype(F32)
    earlier = zero_one(
        row_index(entries, entries) < lax.broadcasted_iota(jnp.int32, (entries, entries), 1)
    )
    before = dot(onehot.astype(BF16), earlier, (1, 0))
    return jnp.sum(before * onehot, axis=0, keepdims=True).astype(jnp.int32)


def scaled_half(grad, gates):
    entries = grad.shape[0]
    weight = jnp.broadcast_to(gates, (entries, entries)).T[:, :1]
    return (weight * grad.astype(F32)).astype(BF16)


def kernel_inputs(
    experts, depth, base,
    ids_hbm, gates_hbm, tokens_hbm, grad_hbm,
    send_hbm, pool_hbm, place_hbm, marks_hbm, scaled_hbm,
    ids, gates, tokens, grad, send, pool, place, marks, scaled, sems,
):
    entries = ids.shape[1]
    half = tokens.shape[1] // 2
    extra = depth - base
    me = lax.axis_index("dp")
    move = Mover(sems)
    small = [move.start(ids_hbm, ids), move.start(gates_hbm, gates)]
    loads = [
        move.start(
            tokens_hbm.at[:, half_at(where, half)], tokens.at[:, pl.ds(part * half, half)]
        )
        for part, where in enumerate((me, 1 - me))
    ]
    grads = move.start(grad_hbm.at[:, half_at(1 - me, half)], grad)
    wait(*small)
    rank = ranks(ids[...], experts)
    over = rank >= base
    kept_slot = jnp.where(over, -1, ids[...] * base + rank)
    into = zero_one(row_index(experts * base, entries) == kept_slot)
    position = jnp.where(over, rank - base, -extra - 1)
    row = row_index(2 * extra, entries)
    stores = []
    pooled = 0.0
    for part in range(2):
        wait(loads[part])
        columns = slice(part * half, (part + 1) * half)
        table = tokens[:, columns]
        send[:, columns] = dot(into, table, (1, 0)).astype(BF16)
        stores.append(
            move.start(
                send.at[:, pl.ds(part * half, half)], send_hbm.at[:, pl.ds(part * half, half)]
            )
        )
        pooled = pooled + dot(zero_one(row == position + part * extra), table, (1, 0))
    pool[...] = with_mark(pooled, jnp.zeros((1, 1), F32))
    place[...] = zero_one(row_index(experts * depth, entries) == ids[...] * depth + rank)
    is_hot = jnp.max(jnp.where(over, ids[...], -1)) == lax.axis_index("expert")
    marks[...] = jnp.broadcast_to(is_hot.astype(F32), marks.shape)
    wait(grads)
    scaled[:entries] = scaled_half(grad[...], gates[...])
    scaled[entries:] = jnp.broadcast_to(
        jnp.concatenate(
            [ids[...].astype(F32), jnp.zeros((1, half - entries), F32)], axis=1
        ),
        (scaled.shape[0] - entries, half),
    ).astype(BF16)
    stores += [
        move.start(source, target)
        for source, target in (
            (scaled, scaled_hbm),
            (pool, pool_hbm),
            (place, place_hbm),
            (marks, marks_hbm),
        )
    ]
    wait(*stores)


def kernel_grads(
    experts, depth, base,
    ids_hbm, gates_hbm, grad_hbm, other_hbm,
    theirs_hbm, own_hbm, pool_hbm,
    ids, gates, grad, other, theirs, own, pool, sems,
):
    entries = ids.shape[1]
    extra = depth - base
    half = grad.shape[1]
    me = lax.axis_index("dp")
    move = Mover(sems)
    loads = [
        move.start(source, target)
        for source, target in (
            (other_hbm, other),
            (ids_hbm, ids),
            (gates_hbm, gates),
            (grad_hbm.at[:, half_at(me, half)], grad),
        )
    ]
    wait(*loads)
    row = row_index(2 * extra, entries)
    pooled, mark = 0.0, 0.0
    stores = []
    for which, target, out in ((1, theirs, theirs_hbm), (0, own, own_hbm)):
        if which == 0:
            of, rows = ids[...], scaled_half(grad[...], gates[...])
        else:
            of = other[entries:, :entries].astype(F32)[:1].astype(jnp.int32)
            rows = other[:entries]
        rank = ranks(of, experts)
        over = rank >= base
        slot = jnp.where(over, -1, of * base + rank)
        position = jnp.where(over, rank - base, -extra - 1)
        target[...] = dot(zero_one(row_index(experts * base, entries) == slot), rows, (1, 0)).astype(BF16)
        stores.append(move.start(target, out))
        pooled = pooled + dot(zero_one(row == position + which * extra), rows, (1, 0))
        crowded = jnp.sum(over.astype(F32), axis=1, keepdims=True) > extra
        mark = mark + crowded.astype(F32)
    pool[...] = with_mark(pooled, mark)
    wait(move.start(pool, pool_hbm), *stores)


def pool_rows(pool, marks, which, extra, half):
    sources = pool.shape[0] // (4 * extra)
    rows = row_index(sources * extra, pool.shape[0])
    columns = lax.broadcasted_iota(jnp.int32, (sources * extra, pool.shape[0]), 1)
    source = lax.shift_right_logical(rows, extra.bit_length() - 1) ^ lax.axis_index("expert")
    target = source * (4 * extra) + which * extra + (rows & (extra - 1))
    select = ((columns == target).astype(F32) * marks[0:1, 0:1]).astype(BF16)
    return dot(select, pool[:, :half], (1, 0)).astype(BF16)


def weight_copies(move, joined, own, other):
    half, hidden = own[0].shape
    return [
        [
            move.start(source, joined.at[pl.ds(at, half), pl.ds(part * hidden, hidden)])
            for part, source in enumerate(pair)
        ]
        for at, pair in ((0, own), (half, other))
    ]


def kernel_base(
    rows_hbm, gate_hbm, up_hbm, other_gate_hbm, other_up_hbm,
    pre_hbm, sent_hbm,
    rows, joined, pre_at, sent, sems,
):
    half = joined.shape[0] // 2
    move = Mover(sems)
    weights = weight_copies(move, joined, (gate_hbm, up_hbm), (other_gate_hbm, other_up_hbm))
    loads = [
        move.start(rows_hbm.at[:, pl.ds(part * half, half)], rows.at[:, pl.ds(part * half, half)])
        for part in range(2)
    ]
    wait(loads[0], *weights[0])
    pre = dot(rows[:, :half], joined[:half], (1, 0))
    wait(loads[1], *weights[1])
    pre = pre + dot(rows[:, half:], joined[half:], (1, 0))
    pre_at[...] = pre
    sent[...] = pre.astype(BF16)
    wait(move.start(sent, sent_hbm), move.start(pre_at, pre_hbm))


def kernel_late(
    extra,
    pool_hbm, marks_hbm, hidden_hbm, gate_hbm, up_hbm, other_gate_hbm, other_up_hbm,
    pre_hbm, late_hbm, packet_hbm,
    pool, marks, joined, pre_at, rows, packet, sems,
):
    half = joined.shape[0] // 2
    both = joined.shape[1]
    late = rows.shape[0]
    move = Mover(sems)
    pooled = [move.start(pool_hbm, pool), move.start(marks_hbm, marks)]
    weights = weight_copies(move, joined, (gate_hbm, up_hbm), (other_gate_hbm, other_up_hbm))
    wait(*pooled)
    rows[...] = pool_rows(pool, marks, 0, extra, half)
    packet[:late] = pool_rows(pool, marks, 1, extra, half)
    stores = [move.start(rows, late_hbm)]
    wait(*weights[0])
    pre = dot(rows[...], joined[:half], (1, 0))
    wait(*weights[1])
    pre = pre + dot(packet[:late], joined[half:], (1, 0))
    pre_at[...] = pre
    stores.append(move.start(pre_at, pre_hbm))
    packet[late : 2 * late, :both] = pre.astype(BF16)
    packet[late : 2 * late, both:] = jnp.zeros((late, half - both), BF16)
    mark = jnp.max(pool[:, half:].astype(F32), axis=0, keepdims=True)[:, :1]
    packet[2 * late :] = jnp.broadcast_to(mark, (packet.shape[0] - 2 * late, half)).astype(BF16)
    stores.append(move.start(packet, packet_hbm))
    wait(*stores)


def kernel_hidden(
    extra,
    recv_hbm, pool_hbm, marks_hbm, down_hbm, _rows_hbm,
    sent_hbm, grads_hbm,
    pool, marks, down, grads, sent, sems,
):
    half = down.shape[1]
    kept = recv_hbm.shape[0]
    move = Mover(sems)
    load = move.start(recv_hbm, grads.at[pl.ds(0, kept)])
    small = [
        move.start(source, target)
        for source, target in ((pool_hbm, pool), (marks_hbm, marks), (down_hbm, down))
    ]
    wait(*small)
    grads[kept:] = pool_rows(pool, marks, 3, extra, half)
    wait(load)
    sent[...] = dot(grads[...], down[...], (1, 1)).astype(BF16)
    wait(move.start(sent, sent_hbm), move.start(grads, grads_hbm))


def kernel_stack(pool_hbm, received_hbm, _one_hbm, _other_hbm, stacked_hbm, pool, sems):
    move = Mover(sems)
    wait(
        *[
            move.start(source, pool.at[:, part])
            for part, source in enumerate((pool_hbm, received_hbm))
        ]
    )
    wait(move.start(pool, stacked_hbm))


def kernel_slot(
    base, depth,
    recv_hbm, pool_hbm, marks_hbm, down_hbm, remote_hbm, pre_hbm, late_pre_hbm,
    gate_hbm, up_hbm, other_gate_hbm, other_up_hbm,
    slot_hbm, act_hbm, sides_hbm, hidden_hbm, grads_hbm,
    pool, marks, down, remote, pre, joined, slot, act, sides, hidden_at, grads, sems,
):
    slots, hidden = act.shape
    half = grads.shape[1]
    extra = depth - base
    kept = recv_hbm.shape[0]
    move = Mover(sems)
    load = move.start(recv_hbm, grads.at[pl.ds(0, kept)])
    first = [
        move.start(source, target)
        for source, target in ((pool_hbm, pool), (marks_hbm, marks), (down_hbm, down))
    ]
    second = [
        move.start(source, target)
        for source, target in (
            (remote_hbm, remote),
            (pre_hbm, pre.at[pl.ds(0, kept)]),
            (late_pre_hbm, pre.at[pl.ds(kept, slots - kept)]),
        )
    ]
    weights = weight_copies(move, joined, (gate_hbm, up_hbm), (other_gate_hbm, other_up_hbm))
    wait(*first)
    grads[kept:] = pool_rows(pool, marks, 2, extra, half)
    wait(load)
    stores = [move.start(grads, grads_hbm)]
    hidden_grad = dot(grads[...], down[...], (1, 1))
    wait(*second)
    hidden_grad = hidden_grad + remote[...].astype(F32)
    hidden_at[...] = hidden_grad.astype(BF16)
    activated, both = sides_of(pre[:, :hidden], pre[:, hidden:], hidden_grad)
    act[...] = activated
    sides[...] = both
    stores += [
        move.start(source, target)
        for source, target in ((hidden_at, hidden_hbm), (act, act_hbm), (sides, sides_hbm))
    ]
    at = lane_row(slots)
    late = at - kept
    target = jnp.where(
        at < kept,
        lax.shift_right_logical(at, base.bit_length() - 1) * depth + (at & (base - 1)),
        lax.shift_right_arithmetic(late, extra.bit_length() - 1) * depth
        + base
        + (late & (extra - 1)),
    )
    order = zero_one(row_index(slots, slots) == target)
    both = dot(order, both, (1, 0)).astype(BF16)
    for part in range(2):
        wait(*weights[part])
        columns = pl.ds(part * half, half)
        slot[:, part * half : (part + 1) * half] = dot(
            both, joined[part * half : (part + 1) * half], (1, 1)
        ).astype(BF16)
        stores.append(move.start(slot.at[:, columns], slot_hbm.at[:, columns]))
    wait(*stores)


def kernel_down(
    pre_hbm, packet_hbm, hidden_hbm, act_hbm, grads_hbm, other_grads_hbm,
    down_hbm, sides_hbm,
    pre, hidden_at, act, grads, other_grads, down, sides, sems,
):
    slots, hidden = act.shape
    kept = pre_hbm.shape[0]
    move = Mover(sems)
    first = [
        move.start(pre_hbm, pre.at[pl.ds(0, kept)]),
        move.start(
            packet_hbm.at[pl.ds(slots - kept, slots - kept), pl.ds(0, 2 * hidden)],
            pre.at[pl.ds(kept, slots - kept)],
        ),
        move.start(hidden_hbm, hidden_at),
    ]
    second = [
        move.start(source, target)
        for source, target in (
            (act_hbm, act),
            (grads_hbm, grads),
            (other_grads_hbm, other_grads),
        )
    ]
    wait(*first)
    act_other, sides_other = sides_of(
        pre[:, :hidden].astype(F32), pre[:, hidden:].astype(F32), hidden_at[...].astype(F32)
    )
    sides[...] = sides_other
    stores = [move.start(sides, sides_hbm)]
    wait(*second)
    down[...] = sum_parts(
        dot(act[...], grads[...], (0, 0)), dot(act_other, other_grads[...], (0, 0))
    )
    stores.append(move.start(down, down_hbm))
    wait(*stores)


def kernel_joined(
    rows_hbm, late_rows_hbm, other_rows_hbm, packet_hbm, sides_hbm, other_sides_hbm,
    gate_hbm, up_hbm,
    rows, other_rows, sides, other_sides, joined, sems,
):
    slots, half = rows.shape
    kept = rows_hbm.shape[0]
    hidden = sides.shape[1] // 2
    base, late = pl.ds(0, kept), pl.ds(kept, slots - kept)
    move = Mover(sems)
    loads = [
        move.start(source, target)
        for source, target in (
            (rows_hbm.at[:, pl.ds(0, half)], rows.at[base]),
            (late_rows_hbm, rows.at[late]),
            (sides_hbm, sides),
            (other_rows_hbm, other_rows.at[base]),
            (packet_hbm.at[pl.ds(0, slots - kept)], other_rows.at[late]),
            (other_sides_hbm, other_sides),
        )
    ]
    wait(*loads)
    stores = []
    for at, target in ((0, gate_hbm), (hidden, up_hbm)):
        columns = slice(at, at + hidden)
        joined[:, columns] = sum_parts(
            dot(rows[...], sides[:, columns], (0, 0)),
            dot(other_rows[...], other_sides[:, columns], (0, 0)),
        )
        stores.append(move.start(joined.at[:, pl.ds(at, hidden)], target))
    wait(*stores)


def kernel_final(
    place_hbm, returned_hbm, own_hbm, other_hbm, input_hbm, down_hbm, place, returned, out, down, sems
):
    half = out.shape[1] // 2
    me = lax.axis_index("dp")
    move = Mover(sems)
    loads = [move.start(place_hbm, place)] + [
        move.start(
            returned_hbm.at[:, pl.ds(part * half, half)], returned.at[:, pl.ds(part * half, half)]
        )
        for part in range(2)
    ]
    at = half_at(me, half), half_at(1 - me, half)
    down_loads = [
        move.start(source, down.at[part]) for part, source in enumerate((own_hbm, other_hbm))
    ]
    wait(*loads[:2])
    stores = []
    for part in range(2):
        columns = slice(part * half, (part + 1) * half)
        out[:, columns] = dot(place[...], returned[:, columns], (0, 0)).astype(BF16)
        stores.append(
            move.start(out.at[:, pl.ds(part * half, half)], input_hbm.at[:, at[part]])
        )
        wait(down_loads[part])
        stores.append(move.start(down.at[part], down_hbm.at[:, at[part]]))
        if part == 0:
            wait(loads[2])
    wait(*stores)


def on_pair(tokens, out_grad, expert_ids, gates, w_gate, w_up, w_down):
    experts = lax.axis_size("expert")
    width = tokens.shape[1]
    per_token = expert_ids.shape[1]
    hidden = w_gate.shape[2]
    entries = expert_ids.size
    depth = 3 * entries // experts
    base = 2 * entries // experts
    extra = depth - base
    slots = experts * depth
    kept = experts * base
    half = width // 2
    late = slots - kept
    ids, weights = expert_ids.reshape(1, entries), gates.reshape(1, entries)
    grad_rows = token_rows(out_grad, per_token)
    int_row, float_row = shape(1, entries, dtype=jnp.int32), shape(1, entries, dtype=F32)
    pool_shape = shape(2 * extra, half + LANES)
    marks_shape = shape(8, LANES, dtype=F32)

    send_inputs, input_pool, place, marks, scaled = call(
        functools.partial(kernel_inputs, experts, depth, base),
        (
            shape(kept, width),
            pool_shape,
            shape(slots, entries),
            marks_shape,
            shape(entries + 16, half),
        ),
        (
            int_row,
            float_row,
            shape(entries, width),
            shape(entries, half),
            shape(kept, width),
            pool_shape,
            shape(slots, entries),
            marks_shape,
            shape(entries + 16, half),
        ),
        11,
        2 * kept * entries * width,
        ids,
        weights,
        token_rows(tokens, per_token),
        grad_rows,
    )
    rows_in = exchange(send_inputs.reshape(experts, base, width), "expert").reshape(kept, width)
    other_scaled = swap(scaled)
    other_gate = swap(w_gate[0])
    rows_half, base_half, by_hidden = shape(slots, half), shape(kept, half), shape(slots, hidden)
    send_theirs, send_own, grad_pool = call(
        functools.partial(kernel_grads, experts, depth, base),
        (base_half, base_half, pool_shape),
        (
            int_row,
            float_row,
            shape(entries, half),
            shape(entries + 16, half),
            base_half,
            base_half,
            pool_shape,
        ),
        7,
        4 * kept * entries * width,
        ids,
        weights,
        grad_rows,
        other_scaled,
    )

    def from_distance(x, distance):
        return lax.ppermute(x, "expert", [(at, at ^ distance) for at in range(experts)])

    step = experts // 4
    pool = jnp.concatenate([input_pool, grad_pool], axis=0)
    pool = jnp.stack([pool] + [from_distance(pool, at * step) for at in range(1, 4)], axis=0)
    rows_in, other_gate, send_theirs, pool = lax.optimization_barrier(
        (rows_in, other_gate, send_theirs, pool)
    )
    grads_theirs = exchange(send_theirs.reshape(experts, base, half), "expert")
    other_weights = other_gate, swap(w_up[0])
    other_rows = swap(rows_in[:, half:])
    own_weights = w_gate[0], w_up[0]
    pre, sent_pre = call(
        kernel_base,
        (shape(kept, 2 * hidden, dtype=F32), shape(kept, 2 * hidden)),
        (
            shape(kept, width),
            shape(width, 2 * hidden),
            shape(kept, 2 * hidden, dtype=F32),
            shape(kept, 2 * hidden),
        ),
        9,
        0,
        rows_in,
        *own_weights,
        *other_weights,
    )
    other_pre = swap(sent_pre)
    while step > 1:
        step //= 2
        early = pool.shape[0] == 4
        (pool,) = call(
            kernel_stack,
            (shape(pool.shape[0], 2, *pool.shape[1:]),),
            (shape(pool.shape[0], 2, *pool.shape[1:]),),
            3,
            LATE_FLOPS if early else 0,
            pool,
            from_distance(pool, step),
            *((other_weights[1], other_weights[0]) if early else (sent_pre, sent_pre)),
        )
        pool = pool.reshape(-1, *pool.shape[2:])
    pool = pool.reshape(-1, half + LANES)
    grads_theirs, send_own, sent_pre = lax.optimization_barrier((grads_theirs, send_own, sent_pre))
    recv_theirs = grads_theirs.reshape(kept, half)
    recv_own = exchange(send_own.reshape(experts, base, half), "expert").reshape(kept, half)

    sent, grads_theirs = call(
        functools.partial(kernel_hidden, extra),
        (by_hidden, rows_half),
        (shape(*pool.shape), marks_shape, shape(hidden, half), rows_half, by_hidden),
        6,
        2 * slots * hidden * half,
        recv_theirs,
        pool,
        marks,
        w_down[0],
        other_rows,
    )
    remote = swap(sent)
    late_pre, late_rows, packet = call(
        functools.partial(kernel_late, extra),
        (
            shape(late, 2 * hidden, dtype=F32),
            shape(late, half),
            shape(2 * late + 16, half),
        ),
        (
            shape(*pool.shape),
            marks_shape,
            shape(width, 2 * hidden),
            shape(late, 2 * hidden, dtype=F32),
            shape(late, half),
            shape(2 * late + 16, half),
        ),
        9,
        4 * late * hidden * width,
        pool,
        marks,
        sent,
        *own_weights,
        *other_weights,
    )
    remote, packet = lax.optimization_barrier((remote, packet))
    other_packet = swap(packet)
    slot_grad, act, sides, hidden_grad, grads_own = call(
        functools.partial(kernel_slot, base, depth),
        (shape(slots, width), by_hidden, shape(slots, 2 * hidden), by_hidden, rows_half),
        (
            shape(*pool.shape),
            marks_shape,
            shape(hidden, half),
            by_hidden,
            shape(slots, 2 * hidden, dtype=F32),
            shape(width, 2 * hidden),
            shape(slots, width),
            by_hidden,
            shape(slots, 2 * hidden),
            by_hidden,
            rows_half,
        ),
        17,
        4 * slots * hidden * width,
        recv_own,
        pool,
        marks,
        w_down[0],
        remote,
        pre,
        late_pre,
        *own_weights,
        *other_weights,
    )
    other_hidden = swap(hidden_grad)
    returned = exchange(slot_grad.reshape(experts, depth, width), "expert").reshape(slots, width)

    own_down, other_sides = call(
        kernel_down,
        (shape(hidden, half), shape(slots, 2 * hidden)),
        (
            shape(slots, 2 * hidden),
            by_hidden,
            by_hidden,
            rows_half,
            rows_half,
            shape(hidden, half),
            shape(slots, 2 * hidden),
        ),
        8,
        LATE_FLOPS,
        other_pre,
        other_packet,
        other_hidden,
        act,
        grads_own,
        grads_theirs,
    )
    other_down = swap(own_down)
    gate_grad, up_grad = call(
        kernel_joined,
        (shape(half, hidden), shape(half, hidden)),
        (
            rows_half,
            rows_half,
            shape(slots, 2 * hidden),
            shape(slots, 2 * hidden),
            shape(half, 2 * hidden),
        ),
        8,
        8 * slots * hidden * half,
        rows_in,
        late_rows,
        other_rows,
        other_packet,
        sides,
        other_sides,
    )
    picked, down_grad = call(
        kernel_final,
        (shape(entries, width), shape(hidden, width)),
        (
            shape(slots, entries),
            shape(slots, width),
            shape(entries, width),
            shape(2, hidden, half),
        ),
        9,
        2 * slots * entries * width,
        place,
        returned,
        own_down,
        other_down,
    )
    crowded = jnp.maximum(jnp.max(packet[2 * late :]), jnp.max(other_packet[2 * late :])) > 0.0
    return crowded, (sum_choices(picked, per_token), gate_grad[None], up_grad[None], down_grad[None])


def on_device(*arguments):
    if lax.axis_size("dp") != 2:
        return on_any(*arguments)
    crowded, results = on_pair(*arguments)
    return lax.while_loop(
        lambda state: state[0], lambda state: (False, on_any(*arguments)), (crowded, results)
    )[1]


def on_any(tokens, out_grad, expert_ids, gates, w_gate, w_up, w_down):
    experts = lax.axis_size("expert")
    width = tokens.shape[1]
    per_token = expert_ids.shape[1]
    hidden = w_gate.shape[2]
    depth = 3 * expert_ids.size // experts
    slots = experts * depth

    pair = lax.axis_size("dp") == 2
    first = lax.axis_index("dp") == 0

    def gather(x, axis):
        if not pair:
            return lax.all_gather(x, "dp", axis=axis, tiled=True)
        other = swap(x)
        return jnp.concatenate([jnp.where(first, x, other), jnp.where(first, other, x)], axis=axis)

    joined = gather(jnp.concatenate([w_gate[0], w_up[0]], axis=1), 0)
    down = gather(w_down[0], 1)
    place = place_matrix(expert_ids, experts, depth)

    def dispatch(table):
        sent = dot(place, table, (1, 0)).astype(BF16).reshape(experts, depth, width)
        return exchange(sent, "expert").reshape(slots, width)

    rows_in = dispatch(token_rows(tokens, per_token))
    grads_in = dispatch(scaled_rows(out_grad, gates))
    preact = dot(rows_in, joined, (1, 0))
    activated, sides = sides_of(
        preact[:, :hidden], preact[:, hidden:], dot(grads_in, down, (1, 1))
    )
    slot_grad = dot(sides, joined, (1, 1)).astype(BF16)
    returned = exchange(slot_grad.reshape(experts, depth, width), "expert").reshape(slots, width)
    down_part = dot(activated, grads_in, (0, 0)).astype(BF16)
    joined_part = dot(rows_in, sides, (0, 0)).astype(BF16)
    if pair:
        low, high = jnp.split(joined_part, 2, axis=0)
        down_grad = sum_parts(down_part, swap(down_part))
        joined_grad = sum_parts(jnp.where(first, low, high), swap(jnp.where(first, high, low)))
    else:
        down_grad = lax.psum(down_part, "dp")
        joined_grad = lax.psum_scatter(joined_part, "dp", scatter_dimension=0, tiled=True)
    input_grad = sum_choices(dot(place, returned, (0, 0)), per_token)
    return (
        input_grad,
        joined_grad[:, :hidden][None],
        joined_grad[:, hidden:][None],
        down_grad[None],
    )


def solution(mesh):
    rows = P(BOTH, None)
    in_specs = (
        rows,
        rows,
        rows,
        rows,
        P("expert", "dp", None),
        P("expert", "dp", None),
        P("expert", None, "dp"),
    )
    out_specs = (
        rows,
        P("expert", "dp", None),
        P("expert", "dp", None),
        P("expert", None, None),
    )
    return jax.shard_map(
        on_device, mesh=mesh, in_specs=in_specs, out_specs=out_specs, check_vma=False
    )
```

```python
import functools

import jax
import jax.numpy as jnp
from jax import lax
from jax.experimental import pallas as pl
from jax.experimental.pallas import tpu as pltpu
from jax.sharding import PartitionSpec as P

BF16 = jnp.bfloat16
F32 = jnp.float32
BOTH = ("dp", "expert")
LATE_FLOPS = 100_000_000_000
LANES = 128


def dot(a, b, contract):
    return lax.dot_general(a, b, ((contract[:1], contract[1:]), ((), ())), preferred_element_type=F32)


def swap(x):
    return lax.ppermute(x, "dp", [(0, 1), (1, 0)])


def exchange(x, axes):
    return lax.all_to_all(x, axes, split_axis=0, concat_axis=0, tiled=True)


def place_matrix(expert_ids, experts, depth):
    entries = expert_ids.size
    flat_ids = expert_ids.reshape(entries)
    order = jnp.arange(entries, dtype=jnp.int32)
    onehot = (flat_ids[:, None] == jnp.arange(experts, dtype=jnp.int32)[None, :]).astype(BF16)
    earlier = (order[None, :] < order[:, None]).astype(BF16)
    before = dot(earlier, onehot, (1, 0))
    ranking = jnp.sum(before * onehot.astype(F32), axis=1).astype(jnp.int32)
    slot_of_entry = flat_ids * depth + ranking
    return (
        jnp.arange(experts * depth, dtype=jnp.int32)[:, None] == slot_of_entry[None, :]
    ).astype(BF16)


def sides_of(gate_pre, up_pre, hidden_grad):
    sigmoid = jax.nn.sigmoid(gate_pre)
    silu_value = gate_pre * sigmoid
    activated = (silu_value * up_pre).astype(BF16)
    gate_side = (hidden_grad * up_pre * sigmoid * (1.0 + gate_pre * (1.0 - sigmoid))).astype(BF16)
    up_side = (hidden_grad * silu_value).astype(BF16)
    return activated, jnp.concatenate([gate_side, up_side], axis=1)


def sum_parts(first, second):
    return (first.astype(BF16).astype(F32) + second.astype(BF16).astype(F32)).astype(BF16)


def scaled_rows(out_grad, gates):
    return (
        (gates[:, :, None] * out_grad.astype(F32)[:, None, :])
        .astype(BF16)
        .reshape(gates.size, out_grad.shape[1])
    )


def token_rows(tokens, per_token):
    return jnp.repeat(tokens, per_token, axis=0) if per_token > 1 else tokens


def sum_choices(picked, per_token):
    if per_token > 1:
        picked = jnp.sum(picked.reshape(-1, per_token, picked.shape[1]).astype(F32), axis=1)
    return picked.astype(BF16)


MIB = 1 << 20
IN_HBM = pl.BlockSpec(memory_space=pltpu.HBM)


def shape(*dims, dtype=BF16):
    return jax.ShapeDtypeStruct(dims, dtype)


def call(kernel, out_shapes, scratch, copies, flops, *operands):
    moved = sum(x.size * x.dtype.itemsize for x in operands)
    moved += sum(x.size * x.dtype.itemsize for x in out_shapes)
    return pl.pallas_call(
        kernel,
        out_shape=list(out_shapes),
        in_specs=[IN_HBM] * len(operands),
        out_specs=[IN_HBM] * len(out_shapes),
        scratch_shapes=[pltpu.VMEM(x.shape, x.dtype) for x in scratch]
        + [pltpu.SemaphoreType.DMA((copies,))],
        compiler_params=pltpu.CompilerParams(vmem_limit_bytes=64 * MIB),
        cost_estimate=pl.CostEstimate(flops=flops, bytes_accessed=moved, transcendentals=0),
    )(*operands)


class Mover:
    def __init__(self, semaphores):
        self.semaphores, self.count = semaphores, 0

    def start(self, source, target):
        copy = pltpu.make_async_copy(source, target, self.semaphores.at[self.count])
        self.count += 1
        copy.start()
        return copy


def wait(*copies):
    for copy in copies:
        copy.wait()


def half_at(index, half):
    return pl.ds(pl.multiple_of(index * half, half), half)


def zero_one(condition):
    return condition.astype(F32).astype(BF16)


def lane_row(count):
    return lax.broadcasted_iota(jnp.int32, (1, count), 1)


def row_index(rows, columns):
    return lax.broadcasted_iota(jnp.int32, (rows, columns), 0)


def with_mark(rows, mark):
    return jnp.concatenate([rows, jnp.broadcast_to(mark, (rows.shape[0], LANES))], axis=1).astype(BF16)


def ranks(ids, experts):
    entries = ids.shape[1]
    onehot = (row_index(experts, entries) == ids).astype(F32)
    earlier = zero_one(
        row_index(entries, entries) < lax.broadcasted_iota(jnp.int32, (entries, entries), 1)
    )
    before = dot(onehot.astype(BF16), earlier, (1, 0))
    return jnp.sum(before * onehot, axis=0, keepdims=True).astype(jnp.int32)


def scaled_half(grad, gates):
    entries = grad.shape[0]
    weight = jnp.broadcast_to(gates, (entries, entries)).T[:, :1]
    return (weight * grad.astype(F32)).astype(BF16)


def kernel_inputs(
    experts, depth, base,
    ids_hbm, gates_hbm, tokens_hbm, grad_hbm,
    send_hbm, pool_hbm, place_hbm, marks_hbm, scaled_hbm,
    ids, gates, tokens, grad, send, pool, place, marks, scaled, sems,
):
    entries = ids.shape[1]
    half = tokens.shape[1] // 2
    extra = depth - base
    me = lax.axis_index("dp")
    move = Mover(sems)
    small = [move.start(ids_hbm, ids), move.start(gates_hbm, gates)]
    loads = [
        move.start(
            tokens_hbm.at[:, half_at(where, half)], tokens.at[:, pl.ds(part * half, half)]
        )
        for part, where in enumerate((me, 1 - me))
    ]
    grads = move.start(grad_hbm.at[:, half_at(1 - me, half)], grad)
    wait(*small)
    rank = ranks(ids[...], experts)
    over = rank >= base
    kept_slot = jnp.where(over, -1, ids[...] * base + rank)
    into = zero_one(row_index(experts * base, entries) == kept_slot)
    position = jnp.where(over, rank - base, -extra - 1)
    row = row_index(2 * extra, entries)
    stores = []
    pooled = 0.0
    for part in range(2):
        wait(loads[part])
        columns = slice(part * half, (part + 1) * half)
        table = tokens[:, columns]
        send[:, columns] = dot(into, table, (1, 0)).astype(BF16)
        stores.append(
            move.start(
                send.at[:, pl.ds(part * half, half)], send_hbm.at[:, pl.ds(part * half, half)]
            )
        )
        pooled = pooled + dot(zero_one(row == position + part * extra), table, (1, 0))
    pool[...] = with_mark(pooled, jnp.zeros((1, 1), F32))
    place[...] = zero_one(row_index(experts * depth, entries) == ids[...] * depth + rank)
    is_hot = jnp.max(jnp.where(over, ids[...], -1)) == lax.axis_index("expert")
    marks[...] = jnp.broadcast_to(is_hot.astype(F32), marks.shape)
    wait(grads)
    scaled[:entries] = scaled_half(grad[...], gates[...])
    scaled[entries:] = jnp.broadcast_to(
        jnp.concatenate(
            [ids[...].astype(F32), jnp.zeros((1, half - entries), F32)], axis=1
        ),
        (scaled.shape[0] - entries, half),
    ).astype(BF16)
    stores += [
        move.start(source, target)
        for source, target in (
            (scaled, scaled_hbm),
            (pool, pool_hbm),
            (place, place_hbm),
            (marks, marks_hbm),
        )
    ]
    wait(*stores)


def kernel_grads(
    experts, depth, base,
    ids_hbm, gates_hbm, grad_hbm, other_hbm,
    theirs_hbm, own_hbm, pool_hbm,
    ids, gates, grad, other, theirs, own, pool, sems,
):
    entries = ids.shape[1]
    extra = depth - base
    half = grad.shape[1]
    me = lax.axis_index("dp")
    move = Mover(sems)
    loads = [
        move.start(source, target)
        for source, target in (
            (other_hbm, other),
            (ids_hbm, ids),
            (gates_hbm, gates),
            (grad_hbm.at[:, half_at(me, half)], grad),
        )
    ]
    wait(*loads)
    row = row_index(2 * extra, entries)
    pooled, mark = 0.0, 0.0
    stores = []
    for which, target, out in ((1, theirs, theirs_hbm), (0, own, own_hbm)):
        if which == 0:
            of, rows = ids[...], scaled_half(grad[...], gates[...])
        else:
            of = other[entries:, :entries].astype(F32)[:1].astype(jnp.int32)
            rows = other[:entries]
        rank = ranks(of, experts)
        over = rank >= base
        slot = jnp.where(over, -1, of * base + rank)
        position = jnp.where(over, rank - base, -extra - 1)
        target[...] = dot(zero_one(row_index(experts * base, entries) == slot), rows, (1, 0)).astype(BF16)
        stores.append(move.start(target, out))
        pooled = pooled + dot(zero_one(row == position + which * extra), rows, (1, 0))
        crowded = jnp.sum(over.astype(F32), axis=1, keepdims=True) > extra
        mark = mark + crowded.astype(F32)
    pool[...] = with_mark(pooled, mark)
    wait(move.start(pool, pool_hbm), *stores)


def weight_copies(move, joined, own, other):
    half, hidden = own[0].shape
    return [
        [
            move.start(source, joined.at[pl.ds(at, half), pl.ds(part * hidden, hidden)])
            for part, source in enumerate(pair)
        ]
        for at, pair in ((0, own), (half, other))
    ]


def kernel_base(
    rows_hbm, gate_hbm, up_hbm, other_gate_hbm, other_up_hbm,
    pre_hbm, sent_hbm,
    rows, joined, pre_at, sent, sems,
):
    half = joined.shape[0] // 2
    move = Mover(sems)
    weights = weight_copies(move, joined, (gate_hbm, up_hbm), (other_gate_hbm, other_up_hbm))
    loads = [
        move.start(rows_hbm.at[:, pl.ds(part * half, half)], rows.at[:, pl.ds(part * half, half)])
        for part in range(2)
    ]
    wait(loads[0], *weights[0])
    pre = dot(rows[:, :half], joined[:half], (1, 0))
    wait(loads[1], *weights[1])
    pre = pre + dot(rows[:, half:], joined[half:], (1, 0))
    pre_at[...] = pre
    sent[...] = pre.astype(BF16)
    wait(move.start(sent, sent_hbm), move.start(pre_at, pre_hbm))


def kernel_late(
    lates_hbm, mark_hbm, base_hbm, _hidden_hbm, gate_hbm, up_hbm, other_gate_hbm, other_up_hbm,
    pre_hbm, sent_hbm, late_hbm, send_hbm,
    mark, joined, pre_at, sent, rows, send, sems,
):
    half = joined.shape[0] // 2
    late = rows.shape[0]
    kept = base_hbm.shape[0]
    move = Mover(sems)
    pooled = [
        move.start(source, target)
        for source, target in (
            (lates_hbm.at[0], rows),
            (lates_hbm.at[1], send),
            (mark_hbm, mark),
        )
    ]
    above = move.start(base_hbm, sent.at[pl.ds(0, kept)])
    weights = weight_copies(move, joined, (gate_hbm, up_hbm), (other_gate_hbm, other_up_hbm))
    wait(*pooled)
    stores = [move.start(rows, late_hbm), move.start(send, send_hbm)]
    wait(*weights[0])
    pre = dot(rows[...], joined[:half], (1, 0))
    wait(*weights[1])
    pre = pre + dot(send[...], joined[half:], (1, 0))
    pre_at[...] = pre
    sent[kept : kept + late] = pre.astype(BF16)
    sent[kept + late :] = jnp.broadcast_to(
        mark[0:1, 0:1], (sent.shape[0] - kept - late, sent.shape[1])
    ).astype(BF16)
    wait(above)
    stores += [move.start(pre_at, pre_hbm), move.start(sent, sent_hbm)]
    wait(*stores)


def kernel_hidden(
    recv_hbm, lates_hbm, down_hbm, _rows_hbm,
    sent_hbm, grads_hbm,
    down, grads, sent, sems,
):
    kept = recv_hbm.shape[0]
    move = Mover(sems)
    wait(
        move.start(recv_hbm, grads.at[pl.ds(0, kept)]),
        move.start(lates_hbm.at[3], grads.at[pl.ds(kept, grads.shape[0] - kept)]),
        move.start(down_hbm, down),
    )
    sent[...] = dot(grads[...], down[...], (1, 1)).astype(BF16)
    wait(move.start(sent, sent_hbm), move.start(grads, grads_hbm))


def kernel_pools(
    extra,
    pool_hbm, received_hbm, marks_hbm, _place_hbm,
    lates_hbm, mark_hbm,
    pool, marks, lates, mark_at, sems,
):
    kinds, late, half = lates.shape
    blocks = pool.shape[0]
    move = Mover(sems)
    wait(
        move.start(marks_hbm, marks),
        *[
            move.start(source, pool.at[:, part])
            for part, source in enumerate((pool_hbm, received_hbm))
        ],
    )
    entries = pool[...].reshape(2 * blocks * kinds * extra, pool.shape[-1])
    total = entries.shape[0]
    rows = row_index(total, 1)
    bits = extra.bit_length() - 1
    kind = lax.shift_right_logical(rows, late.bit_length() - 1)
    source = lax.shift_right_logical(rows & (late - 1), bits) ^ lax.axis_index("expert")
    target = source * (kinds * extra) + kind * extra + (rows & (extra - 1))
    columns = lax.broadcasted_iota(jnp.int32, (total, total), 1)
    select = ((columns == target).astype(F32) * marks[0:1, 0:1]).astype(BF16)
    picked = dot(select, entries[:, :half], (1, 0)).astype(BF16)
    for which in range(kinds):
        lates[which] = picked[which * late : (which + 1) * late]
    mark = jnp.max(entries[:, half:].astype(F32), axis=0, keepdims=True)
    mark_at[...] = jnp.broadcast_to(mark, mark_at.shape)
    wait(move.start(lates, lates_hbm), move.start(mark_at, mark_hbm))


def kernel_stack(pool_hbm, received_hbm, _one_hbm, _other_hbm, stacked_hbm, pool, sems):
    move = Mover(sems)
    wait(
        *[
            move.start(source, pool.at[:, part])
            for part, source in enumerate((pool_hbm, received_hbm))
        ]
    )
    wait(move.start(pool, stacked_hbm))


def kernel_slot(
    base, depth,
    recv_hbm, lates_hbm, down_hbm, remote_hbm, pre_hbm, late_pre_hbm,
    gate_hbm, up_hbm, other_gate_hbm, other_up_hbm,
    slot_hbm, act_hbm, sides_hbm, hidden_hbm, grads_hbm,
    down, remote, pre, joined, slot, act, sides, hidden_at, grads, sems,
):
    slots, hidden = act.shape
    half = grads.shape[1]
    extra = depth - base
    kept = recv_hbm.shape[0]
    move = Mover(sems)
    first = [
        move.start(source, target)
        for source, target in (
            (recv_hbm, grads.at[pl.ds(0, kept)]),
            (lates_hbm.at[2], grads.at[pl.ds(kept, slots - kept)]),
            (down_hbm, down),
        )
    ]
    second = [
        move.start(source, target)
        for source, target in (
            (remote_hbm, remote),
            (pre_hbm, pre.at[pl.ds(0, kept)]),
            (late_pre_hbm, pre.at[pl.ds(kept, slots - kept)]),
        )
    ]
    weights = weight_copies(move, joined, (gate_hbm, up_hbm), (other_gate_hbm, other_up_hbm))
    wait(*first)
    stores = [move.start(grads, grads_hbm)]
    hidden_grad = dot(grads[...], down[...], (1, 1))
    wait(*second)
    hidden_grad = hidden_grad + remote[...].astype(F32)
    hidden_at[...] = hidden_grad.astype(BF16)
    activated, both = sides_of(pre[:, :hidden], pre[:, hidden:], hidden_grad)
    act[...] = activated
    sides[...] = both
    stores += [
        move.start(source, target)
        for source, target in ((hidden_at, hidden_hbm), (act, act_hbm), (sides, sides_hbm))
    ]
    at = lane_row(slots)
    late = at - kept
    target = jnp.where(
        at < kept,
        lax.shift_right_logical(at, base.bit_length() - 1) * depth + (at & (base - 1)),
        lax.shift_right_arithmetic(late, extra.bit_length() - 1) * depth
        + base
        + (late & (extra - 1)),
    )
    order = zero_one(row_index(slots, slots) == target)
    both = dot(order, both, (1, 0)).astype(BF16)
    for part in range(2):
        wait(*weights[part])
        columns = pl.ds(part * half, half)
        slot[:, part * half : (part + 1) * half] = dot(
            both, joined[part * half : (part + 1) * half], (1, 1)
        ).astype(BF16)
        stores.append(move.start(slot.at[:, columns], slot_hbm.at[:, columns]))
    wait(*stores)


def kernel_down(
    pre_hbm, hidden_hbm, act_hbm, grads_hbm, other_grads_hbm,
    down_hbm, sides_hbm,
    pre, hidden_at, act, grads, other_grads, down, sides, sems,
):
    slots, hidden = act.shape
    move = Mover(sems)
    first = [
        move.start(pre_hbm.at[pl.ds(0, slots)], pre),
        move.start(hidden_hbm, hidden_at),
    ]
    second = [
        move.start(source, target)
        for source, target in (
            (act_hbm, act),
            (grads_hbm, grads),
            (other_grads_hbm, other_grads),
        )
    ]
    wait(*first)
    act_other, sides_other = sides_of(
        pre[:, :hidden].astype(F32), pre[:, hidden:].astype(F32), hidden_at[...].astype(F32)
    )
    sides[...] = sides_other
    stores = [move.start(sides, sides_hbm)]
    wait(*second)
    down[...] = sum_parts(
        dot(act[...], grads[...], (0, 0)), dot(act_other, other_grads[...], (0, 0))
    )
    stores.append(move.start(down, down_hbm))
    wait(*stores)


def kernel_joined(
    rows_hbm, late_rows_hbm, other_rows_hbm, other_late_hbm, sides_hbm, other_sides_hbm,
    gate_hbm, up_hbm,
    rows, other_rows, sides, other_sides, joined, sems,
):
    slots, half = rows.shape
    kept = rows_hbm.shape[0]
    hidden = sides.shape[1] // 2
    base, late = pl.ds(0, kept), pl.ds(kept, slots - kept)
    move = Mover(sems)
    loads = [
        move.start(source, target)
        for source, target in (
            (rows_hbm.at[:, pl.ds(0, half)], rows.at[base]),
            (late_rows_hbm, rows.at[late]),
            (sides_hbm, sides),
            (other_rows_hbm, other_rows.at[base]),
            (other_late_hbm, other_rows.at[late]),
            (other_sides_hbm, other_sides),
        )
    ]
    wait(*loads)
    stores = []
    for at, target in ((0, gate_hbm), (hidden, up_hbm)):
        columns = slice(at, at + hidden)
        joined[:, columns] = sum_parts(
            dot(rows[...], sides[:, columns], (0, 0)),
            dot(other_rows[...], other_sides[:, columns], (0, 0)),
        )
        stores.append(move.start(joined.at[:, pl.ds(at, hidden)], target))
    wait(*stores)


def kernel_final(
    place_hbm, returned_hbm, own_hbm, other_hbm, input_hbm, down_hbm, place, returned, out, down, sems
):
    half = out.shape[1] // 2
    me = lax.axis_index("dp")
    move = Mover(sems)
    loads = [move.start(place_hbm, place)] + [
        move.start(
            returned_hbm.at[:, pl.ds(part * half, half)], returned.at[:, pl.ds(part * half, half)]
        )
        for part in range(2)
    ]
    at = half_at(me, half), half_at(1 - me, half)
    down_loads = [
        move.start(source, down.at[part]) for part, source in enumerate((own_hbm, other_hbm))
    ]
    wait(*loads[:2])
    stores = []
    for part in range(2):
        columns = slice(part * half, (part + 1) * half)
        out[:, columns] = dot(place[...], returned[:, columns], (0, 0)).astype(BF16)
        stores.append(
            move.start(out.at[:, pl.ds(part * half, half)], input_hbm.at[:, at[part]])
        )
        wait(down_loads[part])
        stores.append(move.start(down.at[part], down_hbm.at[:, at[part]]))
        if part == 0:
            wait(loads[2])
    wait(*stores)


def on_pair(tokens, out_grad, expert_ids, gates, w_gate, w_up, w_down):
    experts = lax.axis_size("expert")
    width = tokens.shape[1]
    per_token = expert_ids.shape[1]
    hidden = w_gate.shape[2]
    entries = expert_ids.size
    depth = 3 * entries // experts
    base = 2 * entries // experts
    extra = depth - base
    slots = experts * depth
    kept = experts * base
    half = width // 2
    late = slots - kept
    ids, weights = expert_ids.reshape(1, entries), gates.reshape(1, entries)
    grad_rows = token_rows(out_grad, per_token)
    int_row, float_row = shape(1, entries, dtype=jnp.int32), shape(1, entries, dtype=F32)
    pool_shape = shape(2 * extra, half + LANES)
    marks_shape = shape(8, LANES, dtype=F32)

    send_inputs, input_pool, place, marks, scaled = call(
        functools.partial(kernel_inputs, experts, depth, base),
        (
            shape(kept, width),
            pool_shape,
            shape(slots, entries),
            marks_shape,
            shape(entries + 16, half),
        ),
        (
            int_row,
            float_row,
            shape(entries, width),
            shape(entries, half),
            shape(kept, width),
            pool_shape,
            shape(slots, entries),
            marks_shape,
            shape(entries + 16, half),
        ),
        11,
        2 * kept * entries * width,
        ids,
        weights,
        token_rows(tokens, per_token),
        grad_rows,
    )
    rows_in = exchange(send_inputs.reshape(experts, base, width), "expert").reshape(kept, width)
    other_scaled = swap(scaled)
    other_gate = swap(w_gate[0])
    rows_half, base_half, by_hidden = shape(slots, half), shape(kept, half), shape(slots, hidden)
    send_theirs, send_own, grad_pool = call(
        functools.partial(kernel_grads, experts, depth, base),
        (base_half, base_half, pool_shape),
        (
            int_row,
            float_row,
            shape(entries, half),
            shape(entries + 16, half),
            base_half,
            base_half,
            pool_shape,
        ),
        7,
        4 * kept * entries * width,
        ids,
        weights,
        grad_rows,
        other_scaled,
    )

    def from_distance(x, distance):
        return lax.ppermute(x, "expert", [(at, at ^ distance) for at in range(experts)])

    step = experts // 4
    pool = jnp.concatenate([input_pool, grad_pool], axis=0)
    pool = jnp.stack([pool] + [from_distance(pool, at * step) for at in range(1, 4)], axis=0)
    rows_in, other_gate, send_theirs, pool = lax.optimization_barrier(
        (rows_in, other_gate, send_theirs, pool)
    )
    grads_theirs = exchange(send_theirs.reshape(experts, base, half), "expert")
    other_weights = other_gate, swap(w_up[0])
    other_rows = swap(rows_in[:, half:])
    own_weights = w_gate[0], w_up[0]
    pre, sent_pre = call(
        kernel_base,
        (shape(kept, 2 * hidden, dtype=F32), shape(kept, 2 * hidden)),
        (
            shape(kept, width),
            shape(width, 2 * hidden),
            shape(kept, 2 * hidden, dtype=F32),
            shape(kept, 2 * hidden),
        ),
        9,
        0,
        rows_in,
        *own_weights,
        *other_weights,
    )
    step //= 2
    (pool,) = call(
        kernel_stack,
        (shape(4, 2, *pool.shape[1:]),),
        (shape(4, 2, *pool.shape[1:]),),
        3,
        LATE_FLOPS,
        pool,
        from_distance(pool, step),
        other_weights[1],
        other_weights[0],
    )
    pool = pool.reshape(-1, *pool.shape[2:])
    while step > 2:
        step //= 2
        pool = jnp.stack([pool, from_distance(pool, step)], axis=1)
        pool = pool.reshape(-1, *pool.shape[2:])
    late = slots - kept
    lates, mark = call(
        functools.partial(kernel_pools, extra),
        (shape(4, late, half), marks_shape),
        (
            shape(pool.shape[0], 2, *pool.shape[1:]),
            marks_shape,
            shape(4, late, half),
            marks_shape,
        ),
        5,
        0,
        pool,
        from_distance(pool, 1),
        marks,
        sent_pre,
    )
    grads_theirs, send_own, sent_pre = lax.optimization_barrier(
        (grads_theirs, send_own, sent_pre)
    )
    recv_theirs = grads_theirs.reshape(kept, half)
    recv_own = exchange(send_own.reshape(experts, base, half), "expert").reshape(kept, half)

    sent, grads_theirs = call(
        kernel_hidden,
        (by_hidden, rows_half),
        (shape(hidden, half), rows_half, by_hidden),
        5,
        2 * slots * hidden * half,
        recv_theirs,
        lates,
        w_down[0],
        other_rows,
    )
    remote = swap(sent)
    late_pre, sent_late, late_rows, send_late = call(
        kernel_late,
        (
            shape(late, 2 * hidden, dtype=F32),
            shape(slots + 16, 2 * hidden),
            shape(late, half),
            shape(late, half),
        ),
        (
            marks_shape,
            shape(width, 2 * hidden),
            shape(late, 2 * hidden, dtype=F32),
            shape(slots + 16, 2 * hidden),
            shape(late, half),
            shape(late, half),
        ),
        12,
        6_000_000_000,
        lates,
        mark,
        sent_pre,
        sent,
        *own_weights,
        *other_weights,
    )
    other_pre = swap(sent_late)
    slot_grad, act, sides, hidden_grad, grads_own = call(
        functools.partial(kernel_slot, base, depth),
        (shape(slots, width), by_hidden, shape(slots, 2 * hidden), by_hidden, rows_half),
        (
            shape(hidden, half),
            by_hidden,
            shape(slots, 2 * hidden, dtype=F32),
            shape(width, 2 * hidden),
            shape(slots, width),
            by_hidden,
            shape(slots, 2 * hidden),
            by_hidden,
            rows_half,
        ),
        17,
        4 * slots * hidden * width,
        recv_own,
        lates,
        w_down[0],
        remote,
        pre,
        late_pre,
        *own_weights,
        *other_weights,
    )
    other_hidden = swap(hidden_grad)
    hidden_grad, send_late = lax.optimization_barrier((hidden_grad, send_late))
    other_late_rows = swap(send_late)
    returned = exchange(slot_grad.reshape(experts, depth, width), "expert").reshape(slots, width)

    own_down, other_sides = call(
        kernel_down,
        (shape(hidden, half), shape(slots, 2 * hidden)),
        (
            shape(slots, 2 * hidden),
            by_hidden,
            by_hidden,
            rows_half,
            rows_half,
            shape(hidden, half),
            shape(slots, 2 * hidden),
        ),
        8,
        LATE_FLOPS,
        other_pre,
        other_hidden,
        act,
        grads_own,
        grads_theirs,
    )
    own_down, other_late_rows = lax.optimization_barrier((own_down, other_late_rows))
    other_down = swap(own_down)
    gate_grad, up_grad = call(
        kernel_joined,
        (shape(half, hidden), shape(half, hidden)),
        (
            rows_half,
            rows_half,
            shape(slots, 2 * hidden),
            shape(slots, 2 * hidden),
            shape(half, 2 * hidden),
        ),
        8,
        8 * slots * hidden * half,
        rows_in,
        late_rows,
        other_rows,
        other_late_rows,
        sides,
        other_sides,
    )
    picked, down_grad = call(
        kernel_final,
        (shape(entries, width), shape(hidden, width)),
        (
            shape(slots, entries),
            shape(slots, width),
            shape(entries, width),
            shape(2, hidden, half),
        ),
        9,
        2 * slots * entries * width,
        place,
        returned,
        own_down,
        other_down,
    )
    crowded = jnp.maximum(jnp.max(sent_late[slots:]), jnp.max(other_pre[slots:])) > 0.0
    return crowded, (sum_choices(picked, per_token), gate_grad[None], up_grad[None], down_grad[None])


def on_device(*arguments):
    if lax.axis_size("dp") != 2:
        return on_any(*arguments)
    crowded, results = on_pair(*arguments)
    return lax.while_loop(
        lambda state: state[0], lambda state: (False, on_any(*arguments)), (crowded, results)
    )[1]


def on_any(tokens, out_grad, expert_ids, gates, w_gate, w_up, w_down):
    experts = lax.axis_size("expert")
    width = tokens.shape[1]
    per_token = expert_ids.shape[1]
    hidden = w_gate.shape[2]
    depth = 3 * expert_ids.size // experts
    slots = experts * depth

    pair = lax.axis_size("dp") == 2
    first = lax.axis_index("dp") == 0

    def gather(x, axis):
        if not pair:
            return lax.all_gather(x, "dp", axis=axis, tiled=True)
        other = swap(x)
        return jnp.concatenate([jnp.where(first, x, other), jnp.where(first, other, x)], axis=axis)

    joined = gather(jnp.concatenate([w_gate[0], w_up[0]], axis=1), 0)
    down = gather(w_down[0], 1)
    place = place_matrix(expert_ids, experts, depth)

    def dispatch(table):
        sent = dot(place, table, (1, 0)).astype(BF16).reshape(experts, depth, width)
        return exchange(sent, "expert").reshape(slots, width)

    rows_in = dispatch(token_rows(tokens, per_token))
    grads_in = dispatch(scaled_rows(out_grad, gates))
    preact = dot(rows_in, joined, (1, 0))
    activated, sides = sides_of(
        preact[:, :hidden], preact[:, hidden:], dot(grads_in, down, (1, 1))
    )
    slot_grad = dot(sides, joined, (1, 1)).astype(BF16)
    returned = exchange(slot_grad.reshape(experts, depth, width), "expert").reshape(slots, width)
    down_part = dot(activated, grads_in, (0, 0)).astype(BF16)
    joined_part = dot(rows_in, sides, (0, 0)).astype(BF16)
    if pair:
        low, high = jnp.split(joined_part, 2, axis=0)
        down_grad = sum_parts(down_part, swap(down_part))
        joined_grad = sum_parts(jnp.where(first, low, high), swap(jnp.where(first, high, low)))
    else:
        down_grad = lax.psum(down_part, "dp")
        joined_grad = lax.psum_scatter(joined_part, "dp", scatter_dimension=0, tiled=True)
    input_grad = sum_choices(dot(place, returned, (0, 0)), per_token)
    return (
        input_grad,
        joined_grad[:, :hidden][None],
        joined_grad[:, hidden:][None],
        down_grad[None],
    )


def solution(mesh):
    rows = P(BOTH, None)
    in_specs = (
        rows,
        rows,
        rows,
        rows,
        P("expert", "dp", None),
        P("expert", "dp", None),
        P("expert", None, "dp"),
    )
    out_specs = (
        rows,
        P("expert", "dp", None),
        P("expert", "dp", None),
        P("expert", None, None),
    )
    return jax.shard_map(
        on_device, mesh=mesh, in_specs=in_specs, out_specs=out_specs, check_vma=False
    )
```

```python
import functools

import jax
import jax.numpy as jnp
from jax import lax
from jax.experimental import pallas as pl
from jax.experimental.pallas import tpu as pltpu
from jax.sharding import PartitionSpec as P

BF16 = jnp.bfloat16
F32 = jnp.float32
BOTH = ("dp", "expert")
LATE_FLOPS = 100_000_000_000
LANES = 128


def dot(a, b, contract):
    return lax.dot_general(a, b, ((contract[:1], contract[1:]), ((), ())), preferred_element_type=F32)


def swap(x):
    return lax.ppermute(x, "dp", [(0, 1), (1, 0)])


def exchange(x, axes):
    return lax.all_to_all(x, axes, split_axis=0, concat_axis=0, tiled=True)


def place_matrix(expert_ids, experts, depth):
    entries = expert_ids.size
    flat_ids = expert_ids.reshape(entries)
    order = jnp.arange(entries, dtype=jnp.int32)
    onehot = (flat_ids[:, None] == jnp.arange(experts, dtype=jnp.int32)[None, :]).astype(BF16)
    earlier = (order[None, :] < order[:, None]).astype(BF16)
    before = dot(earlier, onehot, (1, 0))
    ranking = jnp.sum(before * onehot.astype(F32), axis=1).astype(jnp.int32)
    slot_of_entry = flat_ids * depth + ranking
    return (
        jnp.arange(experts * depth, dtype=jnp.int32)[:, None] == slot_of_entry[None, :]
    ).astype(BF16)


def sides_of(gate_pre, up_pre, hidden_grad):
    sigmoid = jax.nn.sigmoid(gate_pre)
    silu_value = gate_pre * sigmoid
    activated = (silu_value * up_pre).astype(BF16)
    gate_side = (hidden_grad * up_pre * sigmoid * (1.0 + gate_pre * (1.0 - sigmoid))).astype(BF16)
    up_side = (hidden_grad * silu_value).astype(BF16)
    return activated, jnp.concatenate([gate_side, up_side], axis=1)


def sum_parts(first, second):
    return (first.astype(BF16).astype(F32) + second.astype(BF16).astype(F32)).astype(BF16)


def scaled_rows(out_grad, gates):
    return (
        (gates[:, :, None] * out_grad.astype(F32)[:, None, :])
        .astype(BF16)
        .reshape(gates.size, out_grad.shape[1])
    )


def token_rows(tokens, per_token):
    return jnp.repeat(tokens, per_token, axis=0) if per_token > 1 else tokens


def sum_choices(picked, per_token):
    if per_token > 1:
        picked = jnp.sum(picked.reshape(-1, per_token, picked.shape[1]).astype(F32), axis=1)
    return picked.astype(BF16)


MIB = 1 << 20
IN_HBM = pl.BlockSpec(memory_space=pltpu.HBM)


def shape(*dims, dtype=BF16):
    return jax.ShapeDtypeStruct(dims, dtype)


def call(kernel, out_shapes, scratch, copies, flops, *operands):
    moved = sum(x.size * x.dtype.itemsize for x in operands)
    moved += sum(x.size * x.dtype.itemsize for x in out_shapes)
    return pl.pallas_call(
        kernel,
        out_shape=list(out_shapes),
        in_specs=[IN_HBM] * len(operands),
        out_specs=[IN_HBM] * len(out_shapes),
        scratch_shapes=[pltpu.VMEM(x.shape, x.dtype) for x in scratch]
        + [pltpu.SemaphoreType.DMA((copies,))],
        compiler_params=pltpu.CompilerParams(vmem_limit_bytes=64 * MIB),
        cost_estimate=pl.CostEstimate(flops=flops, bytes_accessed=moved, transcendentals=0),
    )(*operands)


class Mover:
    def __init__(self, semaphores):
        self.semaphores, self.count = semaphores, 0

    def start(self, source, target):
        copy = pltpu.make_async_copy(source, target, self.semaphores.at[self.count])
        self.count += 1
        copy.start()
        return copy


def wait(*copies):
    for copy in copies:
        copy.wait()


def half_at(index, half):
    return pl.ds(pl.multiple_of(index * half, half), half)


def zero_one(condition):
    return condition.astype(F32).astype(BF16)


def lane_row(count):
    return lax.broadcasted_iota(jnp.int32, (1, count), 1)


def row_index(rows, columns):
    return lax.broadcasted_iota(jnp.int32, (rows, columns), 0)


def with_mark(rows, mark):
    return jnp.concatenate([rows, jnp.broadcast_to(mark, (rows.shape[0], LANES))], axis=1).astype(BF16)


def ranks(ids, experts):
    entries = ids.shape[1]
    onehot = (row_index(experts, entries) == ids).astype(F32)
    earlier = zero_one(
        row_index(entries, entries) < lax.broadcasted_iota(jnp.int32, (entries, entries), 1)
    )
    before = dot(onehot.astype(BF16), earlier, (1, 0))
    return jnp.sum(before * onehot, axis=0, keepdims=True).astype(jnp.int32)


def scaled_half(grad, gates):
    entries = grad.shape[0]
    weight = jnp.broadcast_to(gates, (entries, entries)).T[:, :1]
    return (weight * grad.astype(F32)).astype(BF16)


def kernel_inputs(
    experts, depth, base,
    ids_hbm, gates_hbm, tokens_hbm, grad_hbm,
    send_hbm, pool_hbm, place_hbm, marks_hbm, scaled_hbm,
    ids, gates, tokens, grad, send, pool, place, marks, scaled, sems,
):
    entries = ids.shape[1]
    half = tokens.shape[1] // 2
    extra = depth - base
    me = lax.axis_index("dp")
    move = Mover(sems)
    small = [move.start(ids_hbm, ids), move.start(gates_hbm, gates)]
    loads = [
        move.start(
            tokens_hbm.at[:, half_at(where, half)], tokens.at[:, pl.ds(part * half, half)]
        )
        for part, where in enumerate((me, 1 - me))
    ]
    grads = move.start(grad_hbm.at[:, half_at(1 - me, half)], grad)
    wait(*small)
    rank = ranks(ids[...], experts)
    over = rank >= base
    kept_slot = jnp.where(over, -1, ids[...] * base + rank)
    into = zero_one(row_index(experts * base, entries) == kept_slot)
    position = jnp.where(over, rank - base, -extra - 1)
    row = row_index(2 * extra, entries)
    stores = []
    pooled = 0.0
    for part in range(2):
        wait(loads[part])
        columns = slice(part * half, (part + 1) * half)
        table = tokens[:, columns]
        send[:, columns] = dot(into, table, (1, 0)).astype(BF16)
        stores.append(
            move.start(
                send.at[:, pl.ds(part * half, half)], send_hbm.at[:, pl.ds(part * half, half)]
            )
        )
        pooled = pooled + dot(zero_one(row == position + part * extra), table, (1, 0))
    pool[...] = with_mark(pooled, jnp.zeros((1, 1), F32))
    place[...] = zero_one(row_index(experts * depth, entries) == ids[...] * depth + rank)
    is_hot = jnp.max(jnp.where(over, ids[...], -1)) == lax.axis_index("expert")
    marks[...] = jnp.broadcast_to(is_hot.astype(F32), marks.shape)
    wait(grads)
    scaled[:entries] = scaled_half(grad[...], gates[...])
    scaled[entries:] = jnp.broadcast_to(
        jnp.concatenate(
            [ids[...].astype(F32), jnp.zeros((1, half - entries), F32)], axis=1
        ),
        (scaled.shape[0] - entries, half),
    ).astype(BF16)
    stores += [
        move.start(source, target)
        for source, target in (
            (scaled, scaled_hbm),
            (pool, pool_hbm),
            (place, place_hbm),
            (marks, marks_hbm),
        )
    ]
    wait(*stores)


def kernel_grads(
    experts, depth, base,
    ids_hbm, gates_hbm, grad_hbm, other_hbm,
    theirs_hbm, own_hbm, pool_hbm,
    ids, gates, grad, other, theirs, own, pool, sems,
):
    entries = ids.shape[1]
    extra = depth - base
    half = grad.shape[1]
    me = lax.axis_index("dp")
    move = Mover(sems)
    loads = [
        move.start(source, target)
        for source, target in (
            (other_hbm, other),
            (ids_hbm, ids),
            (gates_hbm, gates),
            (grad_hbm.at[:, half_at(me, half)], grad),
        )
    ]
    wait(*loads)
    row = row_index(2 * extra, entries)
    pooled, mark = 0.0, 0.0
    stores = []
    for which, target, out in ((1, theirs, theirs_hbm), (0, own, own_hbm)):
        if which == 0:
            of, rows = ids[...], scaled_half(grad[...], gates[...])
        else:
            of = other[entries:, :entries].astype(F32)[:1].astype(jnp.int32)
            rows = other[:entries]
        rank = ranks(of, experts)
        over = rank >= base
        slot = jnp.where(over, -1, of * base + rank)
        position = jnp.where(over, rank - base, -extra - 1)
        target[...] = dot(zero_one(row_index(experts * base, entries) == slot), rows, (1, 0)).astype(BF16)
        stores.append(move.start(target, out))
        pooled = pooled + dot(zero_one(row == position + which * extra), rows, (1, 0))
        crowded = jnp.sum(over.astype(F32), axis=1, keepdims=True) > extra
        mark = mark + crowded.astype(F32)
    pool[...] = with_mark(pooled, mark)
    wait(move.start(pool, pool_hbm), *stores)


def weight_copies(move, joined, own, other):
    half, hidden = own[0].shape
    return [
        [
            move.start(source, joined.at[pl.ds(at, half), pl.ds(part * hidden, hidden)])
            for part, source in enumerate(pair)
        ]
        for at, pair in ((0, own), (half, other))
    ]


def kernel_base(
    rows_hbm, gate_hbm, up_hbm, other_gate_hbm, other_up_hbm,
    pre_hbm, sent_hbm,
    rows, joined, pre_at, sent, sems,
):
    half = joined.shape[0] // 2
    move = Mover(sems)
    weights = weight_copies(move, joined, (gate_hbm, up_hbm), (other_gate_hbm, other_up_hbm))
    loads = [
        move.start(rows_hbm.at[:, pl.ds(part * half, half)], rows.at[:, pl.ds(part * half, half)])
        for part in range(2)
    ]
    wait(loads[0], *weights[0])
    pre = dot(rows[:, :half], joined[:half], (1, 0))
    wait(loads[1], *weights[1])
    pre = pre + dot(rows[:, half:], joined[half:], (1, 0))
    pre_at[...] = pre
    sent[...] = pre.astype(BF16)
    wait(move.start(sent, sent_hbm), move.start(pre_at, pre_hbm))


def kernel_late(
    lates_hbm, mark_hbm, base_hbm, _hidden_hbm, _rows_hbm, gate_hbm, up_hbm, other_gate_hbm, other_up_hbm,
    pre_hbm, sent_hbm, late_hbm, send_hbm,
    mark, joined, pre_at, sent, rows, send, sems,
):
    half = joined.shape[0] // 2
    late = rows.shape[0]
    kept = base_hbm.shape[0]
    move = Mover(sems)
    pooled = [
        move.start(source, target)
        for source, target in (
            (lates_hbm.at[0], rows),
            (lates_hbm.at[1], send),
            (mark_hbm, mark),
        )
    ]
    above = move.start(base_hbm, sent.at[pl.ds(0, kept)])
    weights = weight_copies(move, joined, (gate_hbm, up_hbm), (other_gate_hbm, other_up_hbm))
    wait(*pooled)
    stores = [move.start(rows, late_hbm), move.start(send, send_hbm)]
    wait(*weights[0])
    pre = dot(rows[...], joined[:half], (1, 0))
    wait(*weights[1])
    pre = pre + dot(send[...], joined[half:], (1, 0))
    pre_at[...] = pre
    sent[kept : kept + late] = pre.astype(BF16)
    sent[kept + late :] = jnp.broadcast_to(
        mark[0:1, 0:1], (sent.shape[0] - kept - late, sent.shape[1])
    ).astype(BF16)
    wait(above)
    stores += [move.start(pre_at, pre_hbm), move.start(sent, sent_hbm)]
    wait(*stores)


def kernel_pools(
    extra,
    pool_hbm, received_hbm, marks_hbm, recv_hbm, down_hbm, _place_hbm,
    sent_hbm, grads_hbm, lates_hbm, mark_hbm,
    pool, marks, lates, mark_at, down, grads, sent, sems,
):
    late, half = lates.shape[1:]
    kinds = lates.shape[0] + 1
    blocks = pool.shape[0]
    kept = recv_hbm.shape[0]
    move = Mover(sems)
    loads = [move.start(recv_hbm, grads.at[pl.ds(0, kept)]), move.start(down_hbm, down)]
    wait(
        move.start(marks_hbm, marks),
        *[
            move.start(source, pool.at[:, part])
            for part, source in enumerate((pool_hbm, received_hbm))
        ],
    )
    entries = pool[...].reshape(2 * blocks * kinds * extra, pool.shape[-1])
    total = entries.shape[0]
    rows = row_index(total, 1)
    bits = extra.bit_length() - 1
    kind = lax.shift_right_logical(rows, late.bit_length() - 1)
    source = lax.shift_right_logical(rows & (late - 1), bits) ^ lax.axis_index("expert")
    target = source * (kinds * extra) + kind * extra + (rows & (extra - 1))
    columns = lax.broadcasted_iota(jnp.int32, (total, total), 1)
    select = ((columns == target).astype(F32) * marks[0:1, 0:1]).astype(BF16)
    picked = dot(select, entries[:, :half], (1, 0)).astype(BF16)
    grads[kept:] = picked[(kinds - 1) * late :]
    wait(*loads)
    sent[...] = dot(grads[...], down[...], (1, 1)).astype(BF16)
    stores = [move.start(sent, sent_hbm), move.start(grads, grads_hbm)]
    for which in range(kinds - 1):
        lates[which] = picked[which * late : (which + 1) * late]
    mark = jnp.max(entries[:, half:].astype(F32), axis=0, keepdims=True)
    mark_at[...] = jnp.broadcast_to(mark, mark_at.shape)
    wait(move.start(lates, lates_hbm), move.start(mark_at, mark_hbm), *stores)


def kernel_stack(pool_hbm, received_hbm, _one_hbm, _other_hbm, stacked_hbm, pool, sems):
    move = Mover(sems)
    wait(
        *[
            move.start(source, pool.at[:, part])
            for part, source in enumerate((pool_hbm, received_hbm))
        ]
    )
    wait(move.start(pool, stacked_hbm))


def kernel_slot(
    base, depth,
    recv_hbm, lates_hbm, down_hbm, remote_hbm, pre_hbm, late_pre_hbm,
    gate_hbm, up_hbm, other_gate_hbm, other_up_hbm,
    slot_hbm, act_hbm, sides_hbm, hidden_hbm, grads_hbm,
    down, remote, pre, joined, slot, act, sides, hidden_at, grads, sems,
):
    slots, hidden = act.shape
    half = grads.shape[1]
    extra = depth - base
    kept = recv_hbm.shape[0]
    move = Mover(sems)
    first = [
        move.start(source, target)
        for source, target in (
            (recv_hbm, grads.at[pl.ds(0, kept)]),
            (lates_hbm.at[2], grads.at[pl.ds(kept, slots - kept)]),
            (down_hbm, down),
        )
    ]
    second = [
        move.start(source, target)
        for source, target in (
            (remote_hbm, remote),
            (pre_hbm, pre.at[pl.ds(0, kept)]),
            (late_pre_hbm, pre.at[pl.ds(kept, slots - kept)]),
        )
    ]
    weights = weight_copies(move, joined, (gate_hbm, up_hbm), (other_gate_hbm, other_up_hbm))
    wait(*first)
    stores = [move.start(grads, grads_hbm)]
    hidden_grad = dot(grads[...], down[...], (1, 1))
    wait(*second)
    hidden_grad = hidden_grad + remote[...].astype(F32)
    hidden_at[...] = hidden_grad.astype(BF16)
    activated, both = sides_of(pre[:, :hidden], pre[:, hidden:], hidden_grad)
    act[...] = activated
    sides[...] = both
    stores += [
        move.start(source, target)
        for source, target in ((hidden_at, hidden_hbm), (act, act_hbm), (sides, sides_hbm))
    ]
    at = lane_row(slots)
    late = at - kept
    target = jnp.where(
        at < kept,
        lax.shift_right_logical(at, base.bit_length() - 1) * depth + (at & (base - 1)),
        lax.shift_right_arithmetic(late, extra.bit_length() - 1) * depth
        + base
        + (late & (extra - 1)),
    )
    order = zero_one(row_index(slots, slots) == target)
    both = dot(order, both, (1, 0)).astype(BF16)
    for part in range(2):
        wait(*weights[part])
        columns = pl.ds(part * half, half)
        slot[:, part * half : (part + 1) * half] = dot(
            both, joined[part * half : (part + 1) * half], (1, 1)
        ).astype(BF16)
        stores.append(move.start(slot.at[:, columns], slot_hbm.at[:, columns]))
    wait(*stores)


def kernel_down(
    pre_hbm, hidden_hbm, act_hbm, grads_hbm, other_grads_hbm,
    down_hbm, sides_hbm,
    pre, hidden_at, act, grads, other_grads, down, sides, sems,
):
    slots, hidden = act.shape
    move = Mover(sems)
    first = [
        move.start(pre_hbm.at[pl.ds(0, slots)], pre),
        move.start(hidden_hbm, hidden_at),
    ]
    second = [
        move.start(source, target)
        for source, target in (
            (act_hbm, act),
            (grads_hbm, grads),
            (other_grads_hbm, other_grads),
        )
    ]
    wait(*first)
    act_other, sides_other = sides_of(
        pre[:, :hidden].astype(F32), pre[:, hidden:].astype(F32), hidden_at[...].astype(F32)
    )
    sides[...] = sides_other
    stores = [move.start(sides, sides_hbm)]
    wait(*second)
    down[...] = sum_parts(
        dot(act[...], grads[...], (0, 0)), dot(act_other, other_grads[...], (0, 0))
    )
    stores.append(move.start(down, down_hbm))
    wait(*stores)


def kernel_joined(
    rows_hbm, late_rows_hbm, other_rows_hbm, other_late_hbm, sides_hbm, other_sides_hbm,
    gate_hbm, up_hbm,
    rows, other_rows, sides, other_sides, joined, sems,
):
    slots, half = rows.shape
    kept = rows_hbm.shape[0]
    hidden = sides.shape[1] // 2
    base, late = pl.ds(0, kept), pl.ds(kept, slots - kept)
    move = Mover(sems)
    loads = [
        move.start(source, target)
        for source, target in (
            (rows_hbm.at[:, pl.ds(0, half)], rows.at[base]),
            (late_rows_hbm, rows.at[late]),
            (sides_hbm, sides),
            (other_rows_hbm, other_rows.at[base]),
            (other_late_hbm, other_rows.at[late]),
            (other_sides_hbm, other_sides),
        )
    ]
    wait(*loads)
    stores = []
    for at, target in ((0, gate_hbm), (hidden, up_hbm)):
        columns = slice(at, at + hidden)
        joined[:, columns] = sum_parts(
            dot(rows[...], sides[:, columns], (0, 0)),
            dot(other_rows[...], other_sides[:, columns], (0, 0)),
        )
        stores.append(move.start(joined.at[:, pl.ds(at, hidden)], target))
    wait(*stores)


def kernel_final(
    place_hbm, returned_hbm, own_hbm, other_hbm, input_hbm, down_hbm, place, returned, out, down, sems
):
    half = out.shape[1] // 2
    me = lax.axis_index("dp")
    move = Mover(sems)
    loads = [move.start(place_hbm, place)] + [
        move.start(
            returned_hbm.at[:, pl.ds(part * half, half)], returned.at[:, pl.ds(part * half, half)]
        )
        for part in range(2)
    ]
    at = half_at(me, half), half_at(1 - me, half)
    down_loads = [
        move.start(source, down.at[part]) for part, source in enumerate((own_hbm, other_hbm))
    ]
    wait(*loads[:2])
    stores = []
    for part in range(2):
        columns = slice(part * half, (part + 1) * half)
        out[:, columns] = dot(place[...], returned[:, columns], (0, 0)).astype(BF16)
        stores.append(
            move.start(out.at[:, pl.ds(part * half, half)], input_hbm.at[:, at[part]])
        )
        wait(down_loads[part])
        stores.append(move.start(down.at[part], down_hbm.at[:, at[part]]))
        if part == 0:
            wait(loads[2])
    wait(*stores)


def on_pair(tokens, out_grad, expert_ids, gates, w_gate, w_up, w_down):
    experts = lax.axis_size("expert")
    width = tokens.shape[1]
    per_token = expert_ids.shape[1]
    hidden = w_gate.shape[2]
    entries = expert_ids.size
    depth = 3 * entries // experts
    base = 2 * entries // experts
    extra = depth - base
    slots = experts * depth
    kept = experts * base
    half = width // 2
    late = slots - kept
    ids, weights = expert_ids.reshape(1, entries), gates.reshape(1, entries)
    grad_rows = token_rows(out_grad, per_token)
    int_row, float_row = shape(1, entries, dtype=jnp.int32), shape(1, entries, dtype=F32)
    pool_shape = shape(2 * extra, half + LANES)
    marks_shape = shape(8, LANES, dtype=F32)

    send_inputs, input_pool, place, marks, scaled = call(
        functools.partial(kernel_inputs, experts, depth, base),
        (
            shape(kept, width),
            pool_shape,
            shape(slots, entries),
            marks_shape,
            shape(entries + 16, half),
        ),
        (
            int_row,
            float_row,
            shape(entries, width),
            shape(entries, half),
            shape(kept, width),
            pool_shape,
            shape(slots, entries),
            marks_shape,
            shape(entries + 16, half),
        ),
        11,
        2 * kept * entries * width,
        ids,
        weights,
        token_rows(tokens, per_token),
        grad_rows,
    )
    rows_in = exchange(send_inputs.reshape(experts, base, width), "expert").reshape(kept, width)
    other_scaled = swap(scaled)
    other_gate = swap(w_gate[0])
    rows_half, base_half, by_hidden = shape(slots, half), shape(kept, half), shape(slots, hidden)
    send_theirs, send_own, grad_pool = call(
        functools.partial(kernel_grads, experts, depth, base),
        (base_half, base_half, pool_shape),
        (
            int_row,
            float_row,
            shape(entries, half),
            shape(entries + 16, half),
            base_half,
            base_half,
            pool_shape,
        ),
        7,
        4 * kept * entries * width,
        ids,
        weights,
        grad_rows,
        other_scaled,
    )

    def from_distance(x, distance):
        return lax.ppermute(x, "expert", [(at, at ^ distance) for at in range(experts)])

    step = experts // 4
    pool = jnp.concatenate([input_pool, grad_pool], axis=0)
    pool = jnp.stack([pool] + [from_distance(pool, at * step) for at in range(1, 4)], axis=0)
    rows_in, other_gate, send_theirs, pool = lax.optimization_barrier(
        (rows_in, other_gate, send_theirs, pool)
    )
    grads_theirs = exchange(send_theirs.reshape(experts, base, half), "expert")
    other_weights = other_gate, swap(w_up[0])
    other_rows = swap(rows_in[:, half:])
    own_weights = w_gate[0], w_up[0]
    pre, sent_pre = call(
        kernel_base,
        (shape(kept, 2 * hidden, dtype=F32), shape(kept, 2 * hidden)),
        (
            shape(kept, width),
            shape(width, 2 * hidden),
            shape(kept, 2 * hidden, dtype=F32),
            shape(kept, 2 * hidden),
        ),
        9,
        0,
        rows_in,
        *own_weights,
        *other_weights,
    )
    step //= 2
    (pool,) = call(
        kernel_stack,
        (shape(4, 2, *pool.shape[1:]),),
        (shape(4, 2, *pool.shape[1:]),),
        3,
        LATE_FLOPS,
        pool,
        from_distance(pool, step),
        other_weights[1],
        other_weights[0],
    )
    pool = pool.reshape(-1, *pool.shape[2:])
    while step > 2:
        step //= 2
        pool = jnp.stack([pool, from_distance(pool, step)], axis=1)
        pool = pool.reshape(-1, *pool.shape[2:])
    late = slots - kept
    other_half_pool = from_distance(pool, 1)
    grads_theirs, send_own, sent_pre = lax.optimization_barrier(
        (grads_theirs, send_own, sent_pre)
    )
    recv_theirs = grads_theirs.reshape(kept, half)
    recv_own = exchange(send_own.reshape(experts, base, half), "expert").reshape(kept, half)

    sent, grads_theirs, lates, mark = call(
        functools.partial(kernel_pools, extra),
        (by_hidden, rows_half, shape(3, late, half), marks_shape),
        (
            shape(pool.shape[0], 2, *pool.shape[1:]),
            marks_shape,
            shape(3, late, half),
            marks_shape,
            shape(hidden, half),
            rows_half,
            by_hidden,
        ),
        9,
        2 * slots * hidden * half,
        pool,
        other_half_pool,
        marks,
        recv_theirs,
        w_down[0],
        sent_pre,
    )
    remote = swap(sent)
    late_pre, sent_late, late_rows, send_late = call(
        kernel_late,
        (
            shape(late, 2 * hidden, dtype=F32),
            shape(slots + 16, 2 * hidden),
            shape(late, half),
            shape(late, half),
        ),
        (
            marks_shape,
            shape(width, 2 * hidden),
            shape(late, 2 * hidden, dtype=F32),
            shape(slots + 16, 2 * hidden),
            shape(late, half),
            shape(late, half),
        ),
        12,
        6_000_000_000,
        lates,
        mark,
        sent_pre,
        sent,
        other_rows,
        *own_weights,
        *other_weights,
    )
    other_pre = swap(sent_late)
    slot_grad, act, sides, hidden_grad, grads_own = call(
        functools.partial(kernel_slot, base, depth),
        (shape(slots, width), by_hidden, shape(slots, 2 * hidden), by_hidden, rows_half),
        (
            shape(hidden, half),
            by_hidden,
            shape(slots, 2 * hidden, dtype=F32),
            shape(width, 2 * hidden),
            shape(slots, width),
            by_hidden,
            shape(slots, 2 * hidden),
            by_hidden,
            rows_half,
        ),
        17,
        4 * slots * hidden * width,
        recv_own,
        lates,
        w_down[0],
        remote,
        pre,
        late_pre,
        *own_weights,
        *other_weights,
    )
    other_hidden = swap(hidden_grad)
    hidden_grad, send_late = lax.optimization_barrier((hidden_grad, send_late))
    other_late_rows = swap(send_late)
    returned = exchange(slot_grad.reshape(experts, depth, width), "expert").reshape(slots, width)

    own_down, other_sides = call(
        kernel_down,
        (shape(hidden, half), shape(slots, 2 * hidden)),
        (
            shape(slots, 2 * hidden),
            by_hidden,
            by_hidden,
            rows_half,
            rows_half,
            shape(hidden, half),
            shape(slots, 2 * hidden),
        ),
        8,
        LATE_FLOPS,
        other_pre,
        other_hidden,
        act,
        grads_own,
        grads_theirs,
    )
    own_down, other_late_rows = lax.optimization_barrier((own_down, other_late_rows))
    other_down = swap(own_down)
    gate_grad, up_grad = call(
        kernel_joined,
        (shape(half, hidden), shape(half, hidden)),
        (
            rows_half,
            rows_half,
            shape(slots, 2 * hidden),
            shape(slots, 2 * hidden),
            shape(half, 2 * hidden),
        ),
        8,
        8 * slots * hidden * half,
        rows_in,
        late_rows,
        other_rows,
        other_late_rows,
        sides,
        other_sides,
    )
    picked, down_grad = call(
        kernel_final,
        (shape(entries, width), shape(hidden, width)),
        (
            shape(slots, entries),
            shape(slots, width),
            shape(entries, width),
            shape(2, hidden, half),
        ),
        9,
        2 * slots * entries * width,
        place,
        returned,
        own_down,
        other_down,
    )
    crowded = jnp.maximum(jnp.max(sent_late[slots:]), jnp.max(other_pre[slots:])) > 0.0
    return crowded, (sum_choices(picked, per_token), gate_grad[None], up_grad[None], down_grad[None])


def on_device(*arguments):
    if lax.axis_size("dp") != 2:
        return on_any(*arguments)
    crowded, results = on_pair(*arguments)
    return lax.while_loop(
        lambda state: state[0], lambda state: (False, on_any(*arguments)), (crowded, results)
    )[1]


def on_any(tokens, out_grad, expert_ids, gates, w_gate, w_up, w_down):
    experts = lax.axis_size("expert")
    width = tokens.shape[1]
    per_token = expert_ids.shape[1]
    hidden = w_gate.shape[2]
    depth = 3 * expert_ids.size // experts
    slots = experts * depth

    pair = lax.axis_size("dp") == 2
    first = lax.axis_index("dp") == 0

    def gather(x, axis):
        if not pair:
            return lax.all_gather(x, "dp", axis=axis, tiled=True)
        other = swap(x)
        return jnp.concatenate([jnp.where(first, x, other), jnp.where(first, other, x)], axis=axis)

    joined = gather(jnp.concatenate([w_gate[0], w_up[0]], axis=1), 0)
    down = gather(w_down[0], 1)
    place = place_matrix(expert_ids, experts, depth)

    def dispatch(table):
        sent = dot(place, table, (1, 0)).astype(BF16).reshape(experts, depth, width)
        return exchange(sent, "expert").reshape(slots, width)

    rows_in = dispatch(token_rows(tokens, per_token))
    grads_in = dispatch(scaled_rows(out_grad, gates))
    preact = dot(rows_in, joined, (1, 0))
    activated, sides = sides_of(
        preact[:, :hidden], preact[:, hidden:], dot(grads_in, down, (1, 1))
    )
    slot_grad = dot(sides, joined, (1, 1)).astype(BF16)
    returned = exchange(slot_grad.reshape(experts, depth, width), "expert").reshape(slots, width)
    down_part = dot(activated, grads_in, (0, 0)).astype(BF16)
    joined_part = dot(rows_in, sides, (0, 0)).astype(BF16)
    if pair:
        low, high = jnp.split(joined_part, 2, axis=0)
        down_grad = sum_parts(down_part, swap(down_part))
        joined_grad = sum_parts(jnp.where(first, low, high), swap(jnp.where(first, high, low)))
    else:
        down_grad = lax.psum(down_part, "dp")
        joined_grad = lax.psum_scatter(joined_part, "dp", scatter_dimension=0, tiled=True)
    input_grad = sum_choices(dot(place, returned, (0, 0)), per_token)
    return (
        input_grad,
        joined_grad[:, :hidden][None],
        joined_grad[:, hidden:][None],
        down_grad[None],
    )


def solution(mesh):
    rows = P(BOTH, None)
    in_specs = (
        rows,
        rows,
        rows,
        rows,
        P("expert", "dp", None),
        P("expert", "dp", None),
        P("expert", None, "dp"),
    )
    out_specs = (
        rows,
        P("expert", "dp", None),
        P("expert", "dp", None),
        P("expert", None, None),
    )
    return jax.shard_map(
        on_device, mesh=mesh, in_specs=in_specs, out_specs=out_specs, check_vma=False
    )
```

```python
import functools

import jax
import jax.numpy as jnp
from jax import lax
from jax.experimental import pallas as pl
from jax.experimental.pallas import tpu as pltpu
from jax.sharding import PartitionSpec as P

BF16 = jnp.bfloat16
F32 = jnp.float32
BOTH = ("dp", "expert")
LATE_FLOPS = 100_000_000_000
LANES = 128


def dot(a, b, contract):
    return lax.dot_general(a, b, ((contract[:1], contract[1:]), ((), ())), preferred_element_type=F32)


def swap(x):
    return lax.ppermute(x, "dp", [(0, 1), (1, 0)])


def exchange(x, axes):
    return lax.all_to_all(x, axes, split_axis=0, concat_axis=0, tiled=True)


def place_matrix(expert_ids, experts, depth):
    entries = expert_ids.size
    flat_ids = expert_ids.reshape(entries)
    order = jnp.arange(entries, dtype=jnp.int32)
    onehot = (flat_ids[:, None] == jnp.arange(experts, dtype=jnp.int32)[None, :]).astype(BF16)
    earlier = (order[None, :] < order[:, None]).astype(BF16)
    before = dot(earlier, onehot, (1, 0))
    ranking = jnp.sum(before * onehot.astype(F32), axis=1).astype(jnp.int32)
    slot_of_entry = flat_ids * depth + ranking
    return (
        jnp.arange(experts * depth, dtype=jnp.int32)[:, None] == slot_of_entry[None, :]
    ).astype(BF16)


def sides_of(gate_pre, up_pre, hidden_grad):
    sigmoid = jax.nn.sigmoid(gate_pre)
    silu_value = gate_pre * sigmoid
    activated = (silu_value * up_pre).astype(BF16)
    gate_side = (hidden_grad * up_pre * sigmoid * (1.0 + gate_pre * (1.0 - sigmoid))).astype(BF16)
    up_side = (hidden_grad * silu_value).astype(BF16)
    return activated, jnp.concatenate([gate_side, up_side], axis=1)


def sum_parts(first, second):
    return (first.astype(BF16).astype(F32) + second.astype(BF16).astype(F32)).astype(BF16)


def scaled_rows(out_grad, gates):
    return (
        (gates[:, :, None] * out_grad.astype(F32)[:, None, :])
        .astype(BF16)
        .reshape(gates.size, out_grad.shape[1])
    )


def token_rows(tokens, per_token):
    return jnp.repeat(tokens, per_token, axis=0) if per_token > 1 else tokens


def sum_choices(picked, per_token):
    if per_token > 1:
        picked = jnp.sum(picked.reshape(-1, per_token, picked.shape[1]).astype(F32), axis=1)
    return picked.astype(BF16)


MIB = 1 << 20
IN_HBM = pl.BlockSpec(memory_space=pltpu.HBM)


def shape(*dims, dtype=BF16):
    return jax.ShapeDtypeStruct(dims, dtype)


def call(kernel, out_shapes, scratch, copies, flops, *operands):
    moved = sum(x.size * x.dtype.itemsize for x in operands)
    moved += sum(x.size * x.dtype.itemsize for x in out_shapes)
    return pl.pallas_call(
        kernel,
        out_shape=list(out_shapes),
        in_specs=[IN_HBM] * len(operands),
        out_specs=[IN_HBM] * len(out_shapes),
        scratch_shapes=[pltpu.VMEM(x.shape, x.dtype) for x in scratch]
        + [pltpu.SemaphoreType.DMA((copies,))],
        compiler_params=pltpu.CompilerParams(vmem_limit_bytes=64 * MIB),
        cost_estimate=pl.CostEstimate(flops=flops, bytes_accessed=moved, transcendentals=0),
    )(*operands)


class Mover:
    def __init__(self, semaphores):
        self.semaphores, self.count = semaphores, 0

    def start(self, source, target):
        copy = pltpu.make_async_copy(source, target, self.semaphores.at[self.count])
        self.count += 1
        copy.start()
        return copy


def wait(*copies):
    for copy in copies:
        copy.wait()


def half_at(index, half):
    return pl.ds(pl.multiple_of(index * half, half), half)


def zero_one(condition):
    return condition.astype(F32).astype(BF16)


def lane_row(count):
    return lax.broadcasted_iota(jnp.int32, (1, count), 1)


def row_index(rows, columns):
    return lax.broadcasted_iota(jnp.int32, (rows, columns), 0)


def with_mark(rows, mark):
    return jnp.concatenate([rows, jnp.broadcast_to(mark, (rows.shape[0], LANES))], axis=1).astype(BF16)


def ranks(ids, experts):
    entries = ids.shape[1]
    onehot = (row_index(experts, entries) == ids).astype(F32)
    earlier = zero_one(
        row_index(entries, entries) < lax.broadcasted_iota(jnp.int32, (entries, entries), 1)
    )
    before = dot(onehot.astype(BF16), earlier, (1, 0))
    return jnp.sum(before * onehot, axis=0, keepdims=True).astype(jnp.int32)


def scaled_half(grad, gates):
    entries = grad.shape[0]
    weight = jnp.broadcast_to(gates, (entries, entries)).T[:, :1]
    return (weight * grad.astype(F32)).astype(BF16)


def kernel_inputs(
    experts, depth, base,
    ids_hbm, gates_hbm, tokens_hbm, grad_hbm,
    send_hbm, pool_hbm, place_hbm, marks_hbm, scaled_hbm,
    ids, gates, tokens, grad, send, pool, place, marks, scaled, sems,
):
    entries = ids.shape[1]
    half = tokens.shape[1] // 2
    extra = depth - base
    me = lax.axis_index("dp")
    move = Mover(sems)
    small = [move.start(ids_hbm, ids), move.start(gates_hbm, gates)]
    loads = [
        move.start(
            tokens_hbm.at[:, half_at(where, half)], tokens.at[:, pl.ds(part * half, half)]
        )
        for part, where in enumerate((me, 1 - me))
    ]
    grads = move.start(grad_hbm.at[:, half_at(1 - me, half)], grad)
    wait(*small)
    rank = ranks(ids[...], experts)
    over = rank >= base
    kept_slot = jnp.where(over, -1, ids[...] * base + rank)
    into = zero_one(row_index(experts * base, entries) == kept_slot)
    position = jnp.where(over, rank - base, -extra - 1)
    row = row_index(2 * extra, entries)
    stores = []
    pooled = 0.0
    for part in range(2):
        wait(loads[part])
        columns = slice(part * half, (part + 1) * half)
        table = tokens[:, columns]
        send[:, columns] = dot(into, table, (1, 0)).astype(BF16)
        stores.append(
            move.start(
                send.at[:, pl.ds(part * half, half)], send_hbm.at[:, pl.ds(part * half, half)]
            )
        )
        pooled = pooled + dot(zero_one(row == position + part * extra), table, (1, 0))
    pool[...] = with_mark(pooled, jnp.zeros((1, 1), F32))
    place[...] = zero_one(row_index(experts * depth, entries) == ids[...] * depth + rank)
    is_hot = jnp.max(jnp.where(over, ids[...], -1)) == lax.axis_index("expert")
    marks[...] = jnp.broadcast_to(is_hot.astype(F32), marks.shape)
    wait(grads)
    scaled[:entries] = scaled_half(grad[...], gates[...])
    scaled[entries:] = jnp.broadcast_to(
        jnp.concatenate(
            [ids[...].astype(F32), jnp.zeros((1, half - entries), F32)], axis=1
        ),
        (scaled.shape[0] - entries, half),
    ).astype(BF16)
    stores += [
        move.start(source, target)
        for source, target in (
            (scaled, scaled_hbm),
            (pool, pool_hbm),
            (place, place_hbm),
            (marks, marks_hbm),
        )
    ]
    wait(*stores)


def kernel_grads(
    experts, depth, base,
    ids_hbm, gates_hbm, grad_hbm, other_hbm,
    theirs_hbm, own_hbm, pool_hbm,
    ids, gates, grad, other, theirs, own, pool, sems,
):
    entries = ids.shape[1]
    extra = depth - base
    half = grad.shape[1]
    me = lax.axis_index("dp")
    move = Mover(sems)
    loads = [
        move.start(source, target)
        for source, target in (
            (other_hbm, other),
            (ids_hbm, ids),
            (gates_hbm, gates),
            (grad_hbm.at[:, half_at(me, half)], grad),
        )
    ]
    wait(*loads)
    row = row_index(2 * extra, entries)
    pooled, mark = 0.0, 0.0
    stores = []
    for which, target, out in ((1, theirs, theirs_hbm), (0, own, own_hbm)):
        if which == 0:
            of, rows = ids[...], scaled_half(grad[...], gates[...])
        else:
            of = other[entries:, :entries].astype(F32)[:1].astype(jnp.int32)
            rows = other[:entries]
        rank = ranks(of, experts)
        over = rank >= base
        slot = jnp.where(over, -1, of * base + rank)
        position = jnp.where(over, rank - base, -extra - 1)
        target[...] = dot(zero_one(row_index(experts * base, entries) == slot), rows, (1, 0)).astype(BF16)
        stores.append(move.start(target, out))
        pooled = pooled + dot(zero_one(row == position + which * extra), rows, (1, 0))
        crowded = jnp.sum(over.astype(F32), axis=1, keepdims=True) > extra
        mark = mark + crowded.astype(F32)
    pool[...] = with_mark(pooled, mark)
    wait(move.start(pool, pool_hbm), *stores)


def weight_copies(move, joined, own, other):
    half, hidden = own[0].shape
    return [
        [
            move.start(source, joined.at[pl.ds(at, half), pl.ds(part * hidden, hidden)])
            for part, source in enumerate(pair)
        ]
        for at, pair in ((0, own), (half, other))
    ]


def kernel_base(
    rows_hbm, gate_hbm, up_hbm, other_gate_hbm, other_up_hbm,
    pre_hbm, sent_hbm,
    rows, joined, pre_at, sent, sems,
):
    half = joined.shape[0] // 2
    move = Mover(sems)
    weights = weight_copies(move, joined, (gate_hbm, up_hbm), (other_gate_hbm, other_up_hbm))
    loads = [
        move.start(rows_hbm.at[:, pl.ds(part * half, half)], rows.at[:, pl.ds(part * half, half)])
        for part in range(2)
    ]
    wait(loads[0], *weights[0])
    pre = dot(rows[:, :half], joined[:half], (1, 0))
    wait(loads[1], *weights[1])
    pre = pre + dot(rows[:, half:], joined[half:], (1, 0))
    pre_at[...] = pre
    sent[...] = pre.astype(BF16)
    wait(move.start(sent, sent_hbm), move.start(pre_at, pre_hbm))


def kernel_late(
    extra,
    pool_hbm, received_hbm, marks_hbm, base_hbm, _hidden_hbm, _rows_hbm, gate_hbm, up_hbm, other_gate_hbm, other_up_hbm,
    pre_hbm, sent_hbm, late_hbm, send_hbm,
    pool, marks, joined, pre_at, sent, rows, send, sems,
):
    half = joined.shape[0] // 2
    late = rows.shape[0]
    kept = base_hbm.shape[0]
    move = Mover(sems)
    pooled = [move.start(marks_hbm, marks), *pool_copies(move, pool, pool_hbm, received_hbm)]
    above = move.start(base_hbm, sent.at[pl.ds(0, kept)])
    weights = weight_copies(move, joined, (gate_hbm, up_hbm), (other_gate_hbm, other_up_hbm))
    wait(*pooled)
    entries = pool[...].reshape(4 * late, pool.shape[-1])
    picked = two_kinds(entries, marks, 0, extra, half)
    rows[...] = picked[:late]
    send[...] = picked[late:]
    mark = jnp.max(entries[:, half:].astype(F32), axis=0, keepdims=True)
    stores = [move.start(rows, late_hbm), move.start(send, send_hbm)]
    wait(*weights[0])
    pre = dot(rows[...], joined[:half], (1, 0))
    wait(*weights[1])
    pre = pre + dot(send[...], joined[half:], (1, 0))
    pre_at[...] = pre
    sent[kept : kept + late] = pre.astype(BF16)
    sent[kept + late :] = jnp.broadcast_to(
        mark[0:1, 0:1], (sent.shape[0] - kept - late, sent.shape[1])
    ).astype(BF16)
    wait(above)
    stores += [move.start(pre_at, pre_hbm), move.start(sent, sent_hbm)]
    wait(*stores)


def pool_copies(move, pool, pool_hbm, received_hbm):
    return [
        move.start(source, pool.at[:, part]) for part, source in enumerate((pool_hbm, received_hbm))
    ]


def two_kinds(entries, marks, first, extra, half):
    late = entries.shape[0] // 4
    rows = row_index(2 * late, 1)
    bits = extra.bit_length() - 1
    kind = first + lax.shift_right_logical(rows, late.bit_length() - 1)
    source = lax.shift_right_logical(rows & (late - 1), bits) ^ lax.axis_index("expert")
    target = source * (4 * extra) + kind * extra + (rows & (extra - 1))
    columns = lax.broadcasted_iota(jnp.int32, (2 * late, 4 * late), 1)
    select = ((columns == target).astype(F32) * marks[0:1, 0:1]).astype(BF16)
    return dot(select, entries[:, :half], (1, 0)).astype(BF16)


def kernel_pools(
    extra,
    pool_hbm, received_hbm, marks_hbm, recv_hbm, down_hbm, _place_hbm,
    sent_hbm, grads_hbm, own_hbm,
    pool, marks, own, down, grads, sent, sems,
):
    late, half = own.shape
    kept = recv_hbm.shape[0]
    move = Mover(sems)
    pooled = [move.start(marks_hbm, marks), *pool_copies(move, pool, pool_hbm, received_hbm)]
    loads = [move.start(recv_hbm, grads.at[pl.ds(0, kept)]), move.start(down_hbm, down)]
    wait(*pooled)
    entries = pool[...].reshape(4 * late, pool.shape[-1])
    picked = two_kinds(entries, marks, 2, extra, half)
    own[...] = picked[:late]
    grads[kept:] = picked[late:]
    stores = [move.start(own, own_hbm)]
    wait(*loads)
    stores.append(move.start(grads, grads_hbm))
    sent[...] = dot(grads[...], down[...], (1, 1)).astype(BF16)
    wait(move.start(sent, sent_hbm), *stores)


def kernel_stack(pool_hbm, received_hbm, _one_hbm, _other_hbm, stacked_hbm, pool, sems):
    move = Mover(sems)
    wait(
        *[
            move.start(source, pool.at[:, part])
            for part, source in enumerate((pool_hbm, received_hbm))
        ]
    )
    wait(move.start(pool, stacked_hbm))


def kernel_slot(
    base, depth,
    recv_hbm, late_hbm, down_hbm, remote_hbm, pre_hbm, late_pre_hbm,
    gate_hbm, up_hbm, other_gate_hbm, other_up_hbm,
    slot_hbm, act_hbm, sides_hbm, hidden_hbm, grads_hbm,
    down, remote, pre, joined, slot, act, sides, hidden_at, grads, sems,
):
    slots, hidden = act.shape
    half = grads.shape[1]
    extra = depth - base
    kept = recv_hbm.shape[0]
    move = Mover(sems)
    first = [
        move.start(source, target)
        for source, target in (
            (recv_hbm, grads.at[pl.ds(0, kept)]),
            (late_hbm, grads.at[pl.ds(kept, slots - kept)]),
            (down_hbm, down),
        )
    ]
    second = [
        move.start(source, target)
        for source, target in (
            (remote_hbm, remote),
            (pre_hbm, pre.at[pl.ds(0, kept)]),
            (late_pre_hbm, pre.at[pl.ds(kept, slots - kept)]),
        )
    ]
    weights = weight_copies(move, joined, (gate_hbm, up_hbm), (other_gate_hbm, other_up_hbm))
    wait(*first)
    stores = [move.start(grads, grads_hbm)]
    hidden_grad = dot(grads[...], down[...], (1, 1))
    wait(*second)
    hidden_grad = hidden_grad + remote[...].astype(F32)
    hidden_at[...] = hidden_grad.astype(BF16)
    activated, both = sides_of(pre[:, :hidden], pre[:, hidden:], hidden_grad)
    act[...] = activated
    sides[...] = both
    stores += [
        move.start(source, target)
        for source, target in ((hidden_at, hidden_hbm), (act, act_hbm), (sides, sides_hbm))
    ]
    at = lane_row(slots)
    late = at - kept
    target = jnp.where(
        at < kept,
        lax.shift_right_logical(at, base.bit_length() - 1) * depth + (at & (base - 1)),
        lax.shift_right_arithmetic(late, extra.bit_length() - 1) * depth
        + base
        + (late & (extra - 1)),
    )
    order = zero_one(row_index(slots, slots) == target)
    both = dot(order, both, (1, 0)).astype(BF16)
    for part in range(2):
        wait(*weights[part])
        columns = pl.ds(part * half, half)
        slot[:, part * half : (part + 1) * half] = dot(
            both, joined[part * half : (part + 1) * half], (1, 1)
        ).astype(BF16)
        stores.append(move.start(slot.at[:, columns], slot_hbm.at[:, columns]))
    wait(*stores)


def kernel_down(
    pre_hbm, hidden_hbm, act_hbm, grads_hbm, other_grads_hbm,
    down_hbm, sides_hbm,
    pre, hidden_at, act, grads, other_grads, down, sides, sems,
):
    slots, hidden = act.shape
    move = Mover(sems)
    first = [
        move.start(pre_hbm.at[pl.ds(0, slots)], pre),
        move.start(hidden_hbm, hidden_at),
    ]
    second = [
        move.start(source, target)
        for source, target in (
            (act_hbm, act),
            (grads_hbm, grads),
            (other_grads_hbm, other_grads),
        )
    ]
    wait(*first)
    act_other, sides_other = sides_of(
        pre[:, :hidden].astype(F32), pre[:, hidden:].astype(F32), hidden_at[...].astype(F32)
    )
    sides[...] = sides_other
    stores = [move.start(sides, sides_hbm)]
    wait(*second)
    down[...] = sum_parts(
        dot(act[...], grads[...], (0, 0)), dot(act_other, other_grads[...], (0, 0))
    )
    stores.append(move.start(down, down_hbm))
    wait(*stores)


def kernel_joined(
    rows_hbm, late_rows_hbm, other_rows_hbm, other_late_hbm, sides_hbm, other_sides_hbm,
    gate_hbm, up_hbm,
    rows, other_rows, sides, other_sides, joined, sems,
):
    slots, half = rows.shape
    kept = rows_hbm.shape[0]
    hidden = sides.shape[1] // 2
    base, late = pl.ds(0, kept), pl.ds(kept, slots - kept)
    move = Mover(sems)
    loads = [
        move.start(source, target)
        for source, target in (
            (rows_hbm.at[:, pl.ds(0, half)], rows.at[base]),
            (late_rows_hbm, rows.at[late]),
            (sides_hbm, sides),
            (other_rows_hbm, other_rows.at[base]),
            (other_late_hbm, other_rows.at[late]),
            (other_sides_hbm, other_sides),
        )
    ]
    wait(*loads)
    stores = []
    for at, target in ((0, gate_hbm), (hidden, up_hbm)):
        columns = slice(at, at + hidden)
        joined[:, columns] = sum_parts(
            dot(rows[...], sides[:, columns], (0, 0)),
            dot(other_rows[...], other_sides[:, columns], (0, 0)),
        )
        stores.append(move.start(joined.at[:, pl.ds(at, hidden)], target))
    wait(*stores)


def kernel_final(
    place_hbm, returned_hbm, own_hbm, other_hbm, input_hbm, down_hbm, place, returned, out, down, sems
):
    half = out.shape[1] // 2
    me = lax.axis_index("dp")
    move = Mover(sems)
    loads = [move.start(place_hbm, place)] + [
        move.start(
            returned_hbm.at[:, pl.ds(part * half, half)], returned.at[:, pl.ds(part * half, half)]
        )
        for part in range(2)
    ]
    at = half_at(me, half), half_at(1 - me, half)
    down_loads = [
        move.start(source, down.at[part]) for part, source in enumerate((own_hbm, other_hbm))
    ]
    wait(*loads[:2])
    stores = []
    for part in range(2):
        columns = slice(part * half, (part + 1) * half)
        out[:, columns] = dot(place[...], returned[:, columns], (0, 0)).astype(BF16)
        stores.append(
            move.start(out.at[:, pl.ds(part * half, half)], input_hbm.at[:, at[part]])
        )
        wait(down_loads[part])
        stores.append(move.start(down.at[part], down_hbm.at[:, at[part]]))
        if part == 0:
            wait(loads[2])
    wait(*stores)


def on_pair(tokens, out_grad, expert_ids, gates, w_gate, w_up, w_down):
    experts = lax.axis_size("expert")
    width = tokens.shape[1]
    per_token = expert_ids.shape[1]
    hidden = w_gate.shape[2]
    entries = expert_ids.size
    depth = 3 * entries // experts
    base = 2 * entries // experts
    extra = depth - base
    slots = experts * depth
    kept = experts * base
    half = width // 2
    late = slots - kept
    ids, weights = expert_ids.reshape(1, entries), gates.reshape(1, entries)
    grad_rows = token_rows(out_grad, per_token)
    int_row, float_row = shape(1, entries, dtype=jnp.int32), shape(1, entries, dtype=F32)
    pool_shape = shape(2 * extra, half + LANES)
    marks_shape = shape(8, LANES, dtype=F32)

    send_inputs, input_pool, place, marks, scaled = call(
        functools.partial(kernel_inputs, experts, depth, base),
        (
            shape(kept, width),
            pool_shape,
            shape(slots, entries),
            marks_shape,
            shape(entries + 16, half),
        ),
        (
            int_row,
            float_row,
            shape(entries, width),
            shape(entries, half),
            shape(kept, width),
            pool_shape,
            shape(slots, entries),
            marks_shape,
            shape(entries + 16, half),
        ),
        11,
        2 * kept * entries * width,
        ids,
        weights,
        token_rows(tokens, per_token),
        grad_rows,
    )
    rows_in = exchange(send_inputs.reshape(experts, base, width), "expert").reshape(kept, width)
    other_scaled = swap(scaled)
    other_gate = swap(w_gate[0])
    rows_half, base_half, by_hidden = shape(slots, half), shape(kept, half), shape(slots, hidden)
    send_theirs, send_own, grad_pool = call(
        functools.partial(kernel_grads, experts, depth, base),
        (base_half, base_half, pool_shape),
        (
            int_row,
            float_row,
            shape(entries, half),
            shape(entries + 16, half),
            base_half,
            base_half,
            pool_shape,
        ),
        7,
        4 * kept * entries * width,
        ids,
        weights,
        grad_rows,
        other_scaled,
    )

    def from_distance(x, distance):
        return lax.ppermute(x, "expert", [(at, at ^ distance) for at in range(experts)])

    step = experts // 4
    pool = jnp.concatenate([input_pool, grad_pool], axis=0)
    pool = jnp.stack([pool] + [from_distance(pool, at * step) for at in range(1, 4)], axis=0)
    rows_in, other_gate, send_theirs, pool = lax.optimization_barrier(
        (rows_in, other_gate, send_theirs, pool)
    )
    grads_theirs = exchange(send_theirs.reshape(experts, base, half), "expert")
    other_weights = other_gate, swap(w_up[0])
    other_rows = swap(rows_in[:, half:])
    own_weights = w_gate[0], w_up[0]
    pre, sent_pre = call(
        kernel_base,
        (shape(kept, 2 * hidden, dtype=F32), shape(kept, 2 * hidden)),
        (
            shape(kept, width),
            shape(width, 2 * hidden),
            shape(kept, 2 * hidden, dtype=F32),
            shape(kept, 2 * hidden),
        ),
        9,
        0,
        rows_in,
        *own_weights,
        *other_weights,
    )
    step //= 2
    (pool,) = call(
        kernel_stack,
        (shape(4, 2, *pool.shape[1:]),),
        (shape(4, 2, *pool.shape[1:]),),
        3,
        LATE_FLOPS,
        pool,
        from_distance(pool, step),
        other_weights[1],
        other_weights[0],
    )
    pool = pool.reshape(-1, *pool.shape[2:])
    while step > 2:
        step //= 2
        pool = jnp.stack([pool, from_distance(pool, step)], axis=1)
        pool = pool.reshape(-1, *pool.shape[2:])
    late = slots - kept
    other_half_pool = from_distance(pool, 1)
    grads_theirs, send_own, sent_pre = lax.optimization_barrier(
        (grads_theirs, send_own, sent_pre)
    )
    recv_theirs = grads_theirs.reshape(kept, half)
    recv_own = exchange(send_own.reshape(experts, base, half), "expert").reshape(kept, half)

    sent, grads_theirs, late_own = call(
        functools.partial(kernel_pools, extra),
        (by_hidden, rows_half, shape(late, half)),
        (
            shape(pool.shape[0], 2, *pool.shape[1:]),
            marks_shape,
            shape(late, half),
            shape(hidden, half),
            rows_half,
            by_hidden,
        ),
        9,
        2 * slots * hidden * half,
        pool,
        other_half_pool,
        marks,
        recv_theirs,
        w_down[0],
        sent_pre,
    )
    remote = swap(sent)
    late_pre, sent_late, late_rows, send_late = call(
        functools.partial(kernel_late, extra),
        (
            shape(late, 2 * hidden, dtype=F32),
            shape(slots + 16, 2 * hidden),
            shape(late, half),
            shape(late, half),
        ),
        (
            shape(pool.shape[0], 2, *pool.shape[1:]),
            marks_shape,
            shape(width, 2 * hidden),
            shape(late, 2 * hidden, dtype=F32),
            shape(slots + 16, 2 * hidden),
            shape(late, half),
            shape(late, half),
        ),
        14,
        6_000_000_000,
        pool,
        other_half_pool,
        marks,
        sent_pre,
        sent,
        other_rows,
        *own_weights,
        *other_weights,
    )
    other_pre = swap(sent_late)
    slot_grad, act, sides, hidden_grad, grads_own = call(
        functools.partial(kernel_slot, base, depth),
        (shape(slots, width), by_hidden, shape(slots, 2 * hidden), by_hidden, rows_half),
        (
            shape(hidden, half),
            by_hidden,
            shape(slots, 2 * hidden, dtype=F32),
            shape(width, 2 * hidden),
            shape(slots, width),
            by_hidden,
            shape(slots, 2 * hidden),
            by_hidden,
            rows_half,
        ),
        17,
        4 * slots * hidden * width,
        recv_own,
        late_own,
        w_down[0],
        remote,
        pre,
        late_pre,
        *own_weights,
        *other_weights,
    )
    other_hidden = swap(hidden_grad)
    hidden_grad, send_late = lax.optimization_barrier((hidden_grad, send_late))
    other_late_rows = swap(send_late)
    returned = exchange(slot_grad.reshape(experts, depth, width), "expert").reshape(slots, width)

    own_down, other_sides = call(
        kernel_down,
        (shape(hidden, half), shape(slots, 2 * hidden)),
        (
            shape(slots, 2 * hidden),
            by_hidden,
            by_hidden,
            rows_half,
            rows_half,
            shape(hidden, half),
            shape(slots, 2 * hidden),
        ),
        8,
        LATE_FLOPS,
        other_pre,
        other_hidden,
        act,
        grads_own,
        grads_theirs,
    )
    own_down, other_late_rows = lax.optimization_barrier((own_down, other_late_rows))
    other_down = swap(own_down)
    gate_grad, up_grad = call(
        kernel_joined,
        (shape(half, hidden), shape(half, hidden)),
        (
            rows_half,
            rows_half,
            shape(slots, 2 * hidden),
            shape(slots, 2 * hidden),
            shape(half, 2 * hidden),
        ),
        8,
        8 * slots * hidden * half,
        rows_in,
        late_rows,
        other_rows,
        other_late_rows,
        sides,
        other_sides,
    )
    picked, down_grad = call(
        kernel_final,
        (shape(entries, width), shape(hidden, width)),
        (
            shape(slots, entries),
            shape(slots, width),
            shape(entries, width),
            shape(2, hidden, half),
        ),
        9,
        2 * slots * entries * width,
        place,
        returned,
        own_down,
        other_down,
    )
    crowded = jnp.maximum(jnp.max(sent_late[slots:]), jnp.max(other_pre[slots:])) > 0.0
    return crowded, (sum_choices(picked, per_token), gate_grad[None], up_grad[None], down_grad[None])


def on_device(*arguments):
    if lax.axis_size("dp") != 2:
        return on_any(*arguments)
    crowded, results = on_pair(*arguments)
    return lax.while_loop(
        lambda state: state[0], lambda state: (False, on_any(*arguments)), (crowded, results)
    )[1]


def on_any(tokens, out_grad, expert_ids, gates, w_gate, w_up, w_down):
    experts = lax.axis_size("expert")
    width = tokens.shape[1]
    per_token = expert_ids.shape[1]
    hidden = w_gate.shape[2]
    depth = 3 * expert_ids.size // experts
    slots = experts * depth

    pair = lax.axis_size("dp") == 2
    first = lax.axis_index("dp") == 0

    def gather(x, axis):
        if not pair:
            return lax.all_gather(x, "dp", axis=axis, tiled=True)
        other = swap(x)
        return jnp.concatenate([jnp.where(first, x, other), jnp.where(first, other, x)], axis=axis)

    joined = gather(jnp.concatenate([w_gate[0], w_up[0]], axis=1), 0)
    down = gather(w_down[0], 1)
    place = place_matrix(expert_ids, experts, depth)

    def dispatch(table):
        sent = dot(place, table, (1, 0)).astype(BF16).reshape(experts, depth, width)
        return exchange(sent, "expert").reshape(slots, width)

    rows_in = dispatch(token_rows(tokens, per_token))
    grads_in = dispatch(scaled_rows(out_grad, gates))
    preact = dot(rows_in, joined, (1, 0))
    activated, sides = sides_of(
        preact[:, :hidden], preact[:, hidden:], dot(grads_in, down, (1, 1))
    )
    slot_grad = dot(sides, joined, (1, 1)).astype(BF16)
    returned = exchange(slot_grad.reshape(experts, depth, width), "expert").reshape(slots, width)
    down_part = dot(activated, grads_in, (0, 0)).astype(BF16)
    joined_part = dot(rows_in, sides, (0, 0)).astype(BF16)
    if pair:
        low, high = jnp.split(joined_part, 2, axis=0)
        down_grad = sum_parts(down_part, swap(down_part))
        joined_grad = sum_parts(jnp.where(first, low, high), swap(jnp.where(first, high, low)))
    else:
        down_grad = lax.psum(down_part, "dp")
        joined_grad = lax.psum_scatter(joined_part, "dp", scatter_dimension=0, tiled=True)
    input_grad = sum_choices(dot(place, returned, (0, 0)), per_token)
    return (
        input_grad,
        joined_grad[:, :hidden][None],
        joined_grad[:, hidden:][None],
        down_grad[None],
    )


def solution(mesh):
    rows = P(BOTH, None)
    in_specs = (
        rows,
        rows,
        rows,
        rows,
        P("expert", "dp", None),
        P("expert", "dp", None),
        P("expert", None, "dp"),
    )
    out_specs = (
        rows,
        P("expert", "dp", None),
        P("expert", "dp", None),
        P("expert", None, None),
    )
    return jax.shard_map(
        on_device, mesh=mesh, in_specs=in_specs, out_specs=out_specs, check_vma=False
    )
```

```python
import functools

import jax
import jax.numpy as jnp
from jax import lax
from jax.experimental import pallas as pl
from jax.experimental.pallas import tpu as pltpu
from jax.sharding import PartitionSpec as P

BF16 = jnp.bfloat16
F32 = jnp.float32
BOTH = ("dp", "expert")
LATE_FLOPS = 100_000_000_000
LANES = 128


def dot(a, b, contract):
    return lax.dot_general(a, b, ((contract[:1], contract[1:]), ((), ())), preferred_element_type=F32)


def swap(x):
    return lax.ppermute(x, "dp", [(0, 1), (1, 0)])


def exchange(x, axes):
    return lax.all_to_all(x, axes, split_axis=0, concat_axis=0, tiled=True)


def place_matrix(expert_ids, experts, depth):
    entries = expert_ids.size
    flat_ids = expert_ids.reshape(entries)
    order = jnp.arange(entries, dtype=jnp.int32)
    onehot = (flat_ids[:, None] == jnp.arange(experts, dtype=jnp.int32)[None, :]).astype(BF16)
    earlier = (order[None, :] < order[:, None]).astype(BF16)
    before = dot(earlier, onehot, (1, 0))
    ranking = jnp.sum(before * onehot.astype(F32), axis=1).astype(jnp.int32)
    slot_of_entry = flat_ids * depth + ranking
    return (
        jnp.arange(experts * depth, dtype=jnp.int32)[:, None] == slot_of_entry[None, :]
    ).astype(BF16)


def sides_of(gate_pre, up_pre, hidden_grad):
    sigmoid = jax.nn.sigmoid(gate_pre)
    silu_value = gate_pre * sigmoid
    activated = (silu_value * up_pre).astype(BF16)
    gate_side = (hidden_grad * up_pre * sigmoid * (1.0 + gate_pre * (1.0 - sigmoid))).astype(BF16)
    up_side = (hidden_grad * silu_value).astype(BF16)
    return activated, jnp.concatenate([gate_side, up_side], axis=1)


def sum_parts(first, second):
    return (first.astype(BF16).astype(F32) + second.astype(BF16).astype(F32)).astype(BF16)


def scaled_rows(out_grad, gates):
    return (
        (gates[:, :, None] * out_grad.astype(F32)[:, None, :])
        .astype(BF16)
        .reshape(gates.size, out_grad.shape[1])
    )


def token_rows(tokens, per_token):
    return jnp.repeat(tokens, per_token, axis=0) if per_token > 1 else tokens


def sum_choices(picked, per_token):
    if per_token > 1:
        picked = jnp.sum(picked.reshape(-1, per_token, picked.shape[1]).astype(F32), axis=1)
    return picked.astype(BF16)


MIB = 1 << 20
IN_HBM = pl.BlockSpec(memory_space=pltpu.HBM)


def shape(*dims, dtype=BF16):
    return jax.ShapeDtypeStruct(dims, dtype)


def call(kernel, out_shapes, scratch, copies, flops, *operands):
    moved = sum(x.size * x.dtype.itemsize for x in operands)
    moved += sum(x.size * x.dtype.itemsize for x in out_shapes)
    return pl.pallas_call(
        kernel,
        out_shape=list(out_shapes),
        in_specs=[IN_HBM] * len(operands),
        out_specs=[IN_HBM] * len(out_shapes),
        scratch_shapes=[pltpu.VMEM(x.shape, x.dtype) for x in scratch]
        + [pltpu.SemaphoreType.DMA((copies,))],
        compiler_params=pltpu.CompilerParams(vmem_limit_bytes=64 * MIB),
        cost_estimate=pl.CostEstimate(flops=flops, bytes_accessed=moved, transcendentals=0),
    )(*operands)


class Mover:
    def __init__(self, semaphores):
        self.semaphores, self.count = semaphores, 0

    def start(self, source, target):
        copy = pltpu.make_async_copy(source, target, self.semaphores.at[self.count])
        self.count += 1
        copy.start()
        return copy


def wait(*copies):
    for copy in copies:
        copy.wait()


def half_at(index, half):
    return pl.ds(pl.multiple_of(index * half, half), half)


def zero_one(condition):
    return condition.astype(F32).astype(BF16)


def lane_row(count):
    return lax.broadcasted_iota(jnp.int32, (1, count), 1)


def row_index(rows, columns):
    return lax.broadcasted_iota(jnp.int32, (rows, columns), 0)


def with_mark(rows, mark):
    return jnp.concatenate([rows, jnp.broadcast_to(mark, (rows.shape[0], LANES))], axis=1).astype(BF16)


def ranks(ids, experts):
    entries = ids.shape[1]
    onehot = (row_index(experts, entries) == ids).astype(F32)
    earlier = zero_one(
        row_index(entries, entries) < lax.broadcasted_iota(jnp.int32, (entries, entries), 1)
    )
    before = dot(onehot.astype(BF16), earlier, (1, 0))
    return jnp.sum(before * onehot, axis=0, keepdims=True).astype(jnp.int32)


def scaled_half(grad, gates):
    entries = grad.shape[0]
    weight = jnp.broadcast_to(gates, (entries, entries)).T[:, :1]
    return (weight * grad.astype(F32)).astype(BF16)


def kernel_inputs(
    experts, depth, base,
    ids_hbm, gates_hbm, tokens_hbm, grad_hbm,
    send_hbm, pool_hbm, place_hbm, marks_hbm, scaled_hbm,
    ids, gates, tokens, grad, send, pool, place, marks, scaled, sems,
):
    entries = ids.shape[1]
    half = tokens.shape[1] // 2
    extra = depth - base
    me = lax.axis_index("dp")
    move = Mover(sems)
    small = [move.start(ids_hbm, ids), move.start(gates_hbm, gates)]
    loads = [
        move.start(
            tokens_hbm.at[:, half_at(where, half)], tokens.at[:, pl.ds(part * half, half)]
        )
        for part, where in enumerate((me, 1 - me))
    ]
    grads = move.start(grad_hbm.at[:, half_at(1 - me, half)], grad)
    wait(*small)
    rank = ranks(ids[...], experts)
    over = rank >= base
    kept_slot = jnp.where(over, -1, ids[...] * base + rank)
    into = zero_one(row_index(experts * base, entries) == kept_slot)
    position = jnp.where(over, rank - base, -extra - 1)
    row = row_index(2 * extra, entries)
    stores = []
    pooled = 0.0
    for part in range(2):
        wait(loads[part])
        columns = slice(part * half, (part + 1) * half)
        table = tokens[:, columns]
        send[:, columns] = dot(into, table, (1, 0)).astype(BF16)
        stores.append(
            move.start(
                send.at[:, pl.ds(part * half, half)], send_hbm.at[:, pl.ds(part * half, half)]
            )
        )
        pooled = pooled + dot(zero_one(row == position + part * extra), table, (1, 0))
    pool[...] = with_mark(pooled, jnp.zeros((1, 1), F32))
    place[...] = zero_one(row_index(experts * depth, entries) == ids[...] * depth + rank)
    is_hot = jnp.max(jnp.where(over, ids[...], -1)) == lax.axis_index("expert")
    marks[...] = jnp.broadcast_to(is_hot.astype(F32), marks.shape)
    wait(grads)
    scaled[:entries] = scaled_half(grad[...], gates[...])
    scaled[entries:] = jnp.broadcast_to(
        jnp.concatenate(
            [ids[...].astype(F32), jnp.zeros((1, half - entries), F32)], axis=1
        ),
        (scaled.shape[0] - entries, half),
    ).astype(BF16)
    stores += [
        move.start(source, target)
        for source, target in (
            (scaled, scaled_hbm),
            (pool, pool_hbm),
            (place, place_hbm),
            (marks, marks_hbm),
        )
    ]
    wait(*stores)


def kernel_grads(
    experts, depth, base,
    ids_hbm, gates_hbm, grad_hbm, other_hbm,
    theirs_hbm, own_hbm, pool_hbm,
    ids, gates, grad, other, theirs, own, pool, sems,
):
    entries = ids.shape[1]
    extra = depth - base
    half = grad.shape[1]
    me = lax.axis_index("dp")
    move = Mover(sems)
    loads = [
        move.start(source, target)
        for source, target in (
            (other_hbm, other),
            (ids_hbm, ids),
            (gates_hbm, gates),
            (grad_hbm.at[:, half_at(me, half)], grad),
        )
    ]
    wait(*loads)
    row = row_index(2 * extra, entries)
    pooled, mark = 0.0, 0.0
    stores = []
    for which, target, out in ((1, theirs, theirs_hbm), (0, own, own_hbm)):
        if which == 0:
            of, rows = ids[...], scaled_half(grad[...], gates[...])
        else:
            of = other[entries:, :entries].astype(F32)[:1].astype(jnp.int32)
            rows = other[:entries]
        rank = ranks(of, experts)
        over = rank >= base
        slot = jnp.where(over, -1, of * base + rank)
        position = jnp.where(over, rank - base, -extra - 1)
        target[...] = dot(zero_one(row_index(experts * base, entries) == slot), rows, (1, 0)).astype(BF16)
        stores.append(move.start(target, out))
        pooled = pooled + dot(zero_one(row == position + which * extra), rows, (1, 0))
        crowded = jnp.sum(over.astype(F32), axis=1, keepdims=True) > extra
        mark = mark + crowded.astype(F32)
    pool[...] = with_mark(pooled, mark)
    wait(move.start(pool, pool_hbm), *stores)


def weight_copies(move, joined, own, other):
    half, hidden = own[0].shape
    return [
        [
            move.start(source, joined.at[pl.ds(at, half), pl.ds(part * hidden, hidden)])
            for part, source in enumerate(pair)
        ]
        for at, pair in ((0, own), (half, other))
    ]


def kernel_base(
    rows_hbm, gate_hbm, up_hbm, other_gate_hbm, other_up_hbm,
    pre_hbm, sent_hbm,
    rows, joined, pre_at, sent, sems,
):
    half = joined.shape[0] // 2
    move = Mover(sems)
    weights = weight_copies(move, joined, (gate_hbm, up_hbm), (other_gate_hbm, other_up_hbm))
    loads = [
        move.start(rows_hbm.at[:, pl.ds(part * half, half)], rows.at[:, pl.ds(part * half, half)])
        for part in range(2)
    ]
    wait(loads[0], *weights[0])
    pre = dot(rows[:, :half], joined[:half], (1, 0))
    wait(loads[1], *weights[1])
    pre = pre + dot(rows[:, half:], joined[half:], (1, 0))
    pre_at[...] = pre
    sent[...] = pre.astype(BF16)
    wait(move.start(sent, sent_hbm), move.start(pre_at, pre_hbm))


def kernel_late(
    extra,
    pool_hbm, received_hbm, marks_hbm, base_hbm, _hidden_hbm, _rows_hbm, gate_hbm, up_hbm, other_gate_hbm, other_up_hbm,
    pre_hbm, sent_hbm, late_hbm, send_hbm,
    pool, marks, joined, pre_at, sent, rows, send, sems,
):
    half = joined.shape[0] // 2
    late = rows.shape[0]
    kept = base_hbm.shape[0]
    move = Mover(sems)
    pooled = [move.start(marks_hbm, marks), *pool_copies(move, pool, pool_hbm, received_hbm)]
    above = move.start(base_hbm, sent.at[pl.ds(0, kept)])
    weights = weight_copies(move, joined, (gate_hbm, up_hbm), (other_gate_hbm, other_up_hbm))
    wait(*pooled)
    entries = pool[...].reshape(4 * late, pool.shape[-1])
    picked = two_kinds(entries, marks, 0, extra, half)
    rows[...] = picked[:late]
    send[...] = picked[late:]
    mark = jnp.max(entries[:, half:].astype(F32), axis=0, keepdims=True)
    stores = [move.start(rows, late_hbm), move.start(send, send_hbm)]
    wait(*weights[0])
    pre = dot(rows[...], joined[:half], (1, 0))
    wait(*weights[1])
    pre = pre + dot(send[...], joined[half:], (1, 0))
    pre_at[...] = pre
    sent[kept : kept + late] = pre.astype(BF16)
    sent[kept + late :] = jnp.broadcast_to(
        mark[0:1, 0:1], (sent.shape[0] - kept - late, sent.shape[1])
    ).astype(BF16)
    wait(above)
    stores += [move.start(pre_at, pre_hbm), move.start(sent, sent_hbm)]
    wait(*stores)


def pool_copies(move, pool, pool_hbm, received_hbm):
    return [
        move.start(source, pool.at[:, part]) for part, source in enumerate((pool_hbm, received_hbm))
    ]


def two_kinds(entries, marks, first, extra, half):
    late = entries.shape[0] // 4
    rows = row_index(2 * late, 1)
    bits = extra.bit_length() - 1
    kind = first + lax.shift_right_logical(rows, late.bit_length() - 1)
    source = lax.shift_right_logical(rows & (late - 1), bits) ^ lax.axis_index("expert")
    target = source * (4 * extra) + kind * extra + (rows & (extra - 1))
    columns = lax.broadcasted_iota(jnp.int32, (2 * late, 4 * late), 1)
    select = ((columns == target).astype(F32) * marks[0:1, 0:1]).astype(BF16)
    return dot(select, entries[:, :half], (1, 0)).astype(BF16)


def kernel_pools(
    extra,
    pool_hbm, received_hbm, marks_hbm, recv_hbm, down_hbm, _place_hbm,
    sent_hbm, grads_hbm, own_hbm,
    pool, marks, own, down, grads, sent, sems,
):
    late, half = own.shape
    kept = recv_hbm.shape[0]
    move = Mover(sems)
    pooled = [move.start(marks_hbm, marks), *pool_copies(move, pool, pool_hbm, received_hbm)]
    loads = [move.start(recv_hbm, grads.at[pl.ds(0, kept)]), move.start(down_hbm, down)]
    wait(*pooled)
    entries = pool[...].reshape(4 * late, pool.shape[-1])
    picked = two_kinds(entries, marks, 2, extra, half)
    own[...] = picked[:late]
    grads[kept:] = picked[late:]
    stores = [move.start(own, own_hbm)]
    wait(*loads)
    stores.append(move.start(grads, grads_hbm))
    sent[...] = dot(grads[...], down[...], (1, 1)).astype(BF16)
    wait(move.start(sent, sent_hbm), *stores)


def kernel_stack(pool_hbm, received_hbm, _one_hbm, _other_hbm, stacked_hbm, pool, sems):
    move = Mover(sems)
    wait(
        *[
            move.start(source, pool.at[:, part])
            for part, source in enumerate((pool_hbm, received_hbm))
        ]
    )
    wait(move.start(pool, stacked_hbm))


def kernel_slot(
    base, depth,
    recv_hbm, late_hbm, down_hbm, remote_hbm, pre_hbm, late_pre_hbm,
    gate_hbm, up_hbm, other_gate_hbm, other_up_hbm,
    slot_hbm, act_hbm, sides_hbm, hidden_hbm, grads_hbm,
    down, remote, pre, joined, slot, act, sides, hidden_at, grads, sems,
):
    slots, hidden = act.shape
    half = grads.shape[1]
    extra = depth - base
    kept = recv_hbm.shape[0]
    move = Mover(sems)
    first = [
        move.start(source, target)
        for source, target in (
            (recv_hbm, grads.at[pl.ds(0, kept)]),
            (late_hbm, grads.at[pl.ds(kept, slots - kept)]),
            (down_hbm, down),
        )
    ]
    second = [
        move.start(source, target)
        for source, target in (
            (remote_hbm, remote),
            (pre_hbm, pre.at[pl.ds(0, kept)]),
            (late_pre_hbm, pre.at[pl.ds(kept, slots - kept)]),
        )
    ]
    weights = weight_copies(move, joined, (gate_hbm, up_hbm), (other_gate_hbm, other_up_hbm))
    at = lane_row(slots)
    late = at - kept
    target = jnp.where(
        at < kept,
        lax.shift_right_logical(at, base.bit_length() - 1) * depth + (at & (base - 1)),
        lax.shift_right_arithmetic(late, extra.bit_length() - 1) * depth
        + base
        + (late & (extra - 1)),
    )
    order = zero_one(row_index(slots, slots) == target)
    wait(*first)
    stores = [move.start(grads, grads_hbm)]
    hidden_grad = dot(grads[...], down[...], (1, 1))
    wait(*second)
    hidden_grad = hidden_grad + remote[...].astype(F32)
    hidden_at[...] = hidden_grad.astype(BF16)
    activated, both = sides_of(pre[:, :hidden], pre[:, hidden:], hidden_grad)
    act[...] = activated
    sides[...] = both
    stores += [
        move.start(source, target)
        for source, target in ((hidden_at, hidden_hbm), (act, act_hbm), (sides, sides_hbm))
    ]
    both = dot(order, both, (1, 0)).astype(BF16)
    for part in range(2):
        wait(*weights[part])
        columns = pl.ds(part * half, half)
        slot[:, part * half : (part + 1) * half] = dot(
            both, joined[part * half : (part + 1) * half], (1, 1)
        ).astype(BF16)
        stores.append(move.start(slot.at[:, columns], slot_hbm.at[:, columns]))
    wait(*stores)


def kernel_down(
    pre_hbm, hidden_hbm, act_hbm, grads_hbm, other_grads_hbm,
    down_hbm, sides_hbm,
    pre, hidden_at, act, grads, other_grads, down, sides, sems,
):
    slots, hidden = act.shape
    move = Mover(sems)
    first = [
        move.start(pre_hbm.at[pl.ds(0, slots)], pre),
        move.start(hidden_hbm, hidden_at),
    ]
    second = [
        move.start(source, target)
        for source, target in (
            (act_hbm, act),
            (grads_hbm, grads),
            (other_grads_hbm, other_grads),
        )
    ]
    wait(*first)
    act_other, sides_other = sides_of(
        pre[:, :hidden].astype(F32), pre[:, hidden:].astype(F32), hidden_at[...].astype(F32)
    )
    sides[...] = sides_other
    stores = [move.start(sides, sides_hbm)]
    wait(*second)
    down[...] = sum_parts(
        dot(act[...], grads[...], (0, 0)), dot(act_other, other_grads[...], (0, 0))
    )
    stores.append(move.start(down, down_hbm))
    wait(*stores)


def kernel_joined(
    rows_hbm, late_rows_hbm, other_rows_hbm, other_late_hbm, sides_hbm, other_sides_hbm,
    gate_hbm, up_hbm,
    rows, other_rows, sides, other_sides, joined, sems,
):
    slots, half = rows.shape
    kept = rows_hbm.shape[0]
    hidden = sides.shape[1] // 2
    base, late = pl.ds(0, kept), pl.ds(kept, slots - kept)
    move = Mover(sems)
    loads = [
        move.start(source, target)
        for source, target in (
            (rows_hbm.at[:, pl.ds(0, half)], rows.at[base]),
            (late_rows_hbm, rows.at[late]),
            (sides_hbm, sides),
            (other_rows_hbm, other_rows.at[base]),
            (other_late_hbm, other_rows.at[late]),
            (other_sides_hbm, other_sides),
        )
    ]
    wait(*loads)
    stores = []
    for at, target in ((0, gate_hbm), (hidden, up_hbm)):
        columns = slice(at, at + hidden)
        joined[:, columns] = sum_parts(
            dot(rows[...], sides[:, columns], (0, 0)),
            dot(other_rows[...], other_sides[:, columns], (0, 0)),
        )
        stores.append(move.start(joined.at[:, pl.ds(at, hidden)], target))
    wait(*stores)


def kernel_final(
    place_hbm, returned_hbm, own_hbm, other_hbm, input_hbm, down_hbm, place, returned, out, down, sems
):
    half = out.shape[1] // 2
    me = lax.axis_index("dp")
    move = Mover(sems)
    loads = [move.start(place_hbm, place)] + [
        move.start(
            returned_hbm.at[:, pl.ds(part * half, half)], returned.at[:, pl.ds(part * half, half)]
        )
        for part in range(2)
    ]
    at = half_at(me, half), half_at(1 - me, half)
    down_loads = [
        move.start(source, down.at[part]) for part, source in enumerate((own_hbm, other_hbm))
    ]
    wait(*loads[:2])
    stores = []
    for part in range(2):
        columns = slice(part * half, (part + 1) * half)
        out[:, columns] = dot(place[...], returned[:, columns], (0, 0)).astype(BF16)
        stores.append(
            move.start(out.at[:, pl.ds(part * half, half)], input_hbm.at[:, at[part]])
        )
        wait(down_loads[part])
        stores.append(move.start(down.at[part], down_hbm.at[:, at[part]]))
        if part == 0:
            wait(loads[2])
    wait(*stores)


def on_pair(tokens, out_grad, expert_ids, gates, w_gate, w_up, w_down):
    experts = lax.axis_size("expert")
    width = tokens.shape[1]
    per_token = expert_ids.shape[1]
    hidden = w_gate.shape[2]
    entries = expert_ids.size
    depth = 3 * entries // experts
    base = 2 * entries // experts
    extra = depth - base
    slots = experts * depth
    kept = experts * base
    half = width // 2
    late = slots - kept
    ids, weights = expert_ids.reshape(1, entries), gates.reshape(1, entries)
    grad_rows = token_rows(out_grad, per_token)
    int_row, float_row = shape(1, entries, dtype=jnp.int32), shape(1, entries, dtype=F32)
    pool_shape = shape(2 * extra, half + LANES)
    marks_shape = shape(8, LANES, dtype=F32)

    send_inputs, input_pool, place, marks, scaled = call(
        functools.partial(kernel_inputs, experts, depth, base),
        (
            shape(kept, width),
            pool_shape,
            shape(slots, entries),
            marks_shape,
            shape(entries + 16, half),
        ),
        (
            int_row,
            float_row,
            shape(entries, width),
            shape(entries, half),
            shape(kept, width),
            pool_shape,
            shape(slots, entries),
            marks_shape,
            shape(entries + 16, half),
        ),
        11,
        2 * kept * entries * width,
        ids,
        weights,
        token_rows(tokens, per_token),
        grad_rows,
    )
    rows_in = exchange(send_inputs.reshape(experts, base, width), "expert").reshape(kept, width)
    other_scaled = swap(scaled)
    other_gate = swap(w_gate[0])
    rows_half, base_half, by_hidden = shape(slots, half), shape(kept, half), shape(slots, hidden)
    send_theirs, send_own, grad_pool = call(
        functools.partial(kernel_grads, experts, depth, base),
        (base_half, base_half, pool_shape),
        (
            int_row,
            float_row,
            shape(entries, half),
            shape(entries + 16, half),
            base_half,
            base_half,
            pool_shape,
        ),
        7,
        4 * kept * entries * width,
        ids,
        weights,
        grad_rows,
        other_scaled,
    )

    def from_distance(x, distance):
        return lax.ppermute(x, "expert", [(at, at ^ distance) for at in range(experts)])

    step = experts // 4
    pool = jnp.concatenate([input_pool, grad_pool], axis=0)
    pool = jnp.stack([pool] + [from_distance(pool, at * step) for at in range(1, 4)], axis=0)
    rows_in, other_gate, send_theirs, pool = lax.optimization_barrier(
        (rows_in, other_gate, send_theirs, pool)
    )
    grads_theirs = exchange(send_theirs.reshape(experts, base, half), "expert")
    other_weights = other_gate, swap(w_up[0])
    other_rows = swap(rows_in[:, half:])
    own_weights = w_gate[0], w_up[0]
    pre, sent_pre = call(
        kernel_base,
        (shape(kept, 2 * hidden, dtype=F32), shape(kept, 2 * hidden)),
        (
            shape(kept, width),
            shape(width, 2 * hidden),
            shape(kept, 2 * hidden, dtype=F32),
            shape(kept, 2 * hidden),
        ),
        9,
        0,
        rows_in,
        *own_weights,
        *other_weights,
    )
    step //= 2
    (pool,) = call(
        kernel_stack,
        (shape(4, 2, *pool.shape[1:]),),
        (shape(4, 2, *pool.shape[1:]),),
        3,
        LATE_FLOPS,
        pool,
        from_distance(pool, step),
        other_weights[1],
        other_weights[0],
    )
    pool = pool.reshape(-1, *pool.shape[2:])
    while step > 2:
        step //= 2
        pool = jnp.stack([pool, from_distance(pool, step)], axis=1)
        pool = pool.reshape(-1, *pool.shape[2:])
    late = slots - kept
    other_half_pool = from_distance(pool, 1)
    grads_theirs, send_own, sent_pre = lax.optimization_barrier(
        (grads_theirs, send_own, sent_pre)
    )
    recv_theirs = grads_theirs.reshape(kept, half)
    recv_own = exchange(send_own.reshape(experts, base, half), "expert").reshape(kept, half)

    sent, grads_theirs, late_own = call(
        functools.partial(kernel_pools, extra),
        (by_hidden, rows_half, shape(late, half)),
        (
            shape(pool.shape[0], 2, *pool.shape[1:]),
            marks_shape,
            shape(late, half),
            shape(hidden, half),
            rows_half,
            by_hidden,
        ),
        9,
        2 * slots * hidden * half,
        pool,
        other_half_pool,
        marks,
        recv_theirs,
        w_down[0],
        sent_pre,
    )
    remote = swap(sent)
    late_pre, sent_late, late_rows, send_late = call(
        functools.partial(kernel_late, extra),
        (
            shape(late, 2 * hidden, dtype=F32),
            shape(slots + 16, 2 * hidden),
            shape(late, half),
            shape(late, half),
        ),
        (
            shape(pool.shape[0], 2, *pool.shape[1:]),
            marks_shape,
            shape(width, 2 * hidden),
            shape(late, 2 * hidden, dtype=F32),
            shape(slots + 16, 2 * hidden),
            shape(late, half),
            shape(late, half),
        ),
        14,
        6_000_000_000,
        pool,
        other_half_pool,
        marks,
        sent_pre,
        sent,
        other_rows,
        *own_weights,
        *other_weights,
    )
    other_pre = swap(sent_late)
    slot_grad, act, sides, hidden_grad, grads_own = call(
        functools.partial(kernel_slot, base, depth),
        (shape(slots, width), by_hidden, shape(slots, 2 * hidden), by_hidden, rows_half),
        (
            shape(hidden, half),
            by_hidden,
            shape(slots, 2 * hidden, dtype=F32),
            shape(width, 2 * hidden),
            shape(slots, width),
            by_hidden,
            shape(slots, 2 * hidden),
            by_hidden,
            rows_half,
        ),
        17,
        4 * slots * hidden * width,
        recv_own,
        late_own,
        w_down[0],
        remote,
        pre,
        late_pre,
        *own_weights,
        *other_weights,
    )
    other_hidden = swap(hidden_grad)
    hidden_grad, send_late = lax.optimization_barrier((hidden_grad, send_late))
    other_late_rows = swap(send_late)
    returned = exchange(slot_grad.reshape(experts, depth, width), "expert").reshape(slots, width)

    own_down, other_sides = call(
        kernel_down,
        (shape(hidden, half), shape(slots, 2 * hidden)),
        (
            shape(slots, 2 * hidden),
            by_hidden,
            by_hidden,
            rows_half,
            rows_half,
            shape(hidden, half),
            shape(slots, 2 * hidden),
        ),
        8,
        LATE_FLOPS,
        other_pre,
        other_hidden,
        act,
        grads_own,
        grads_theirs,
    )
    own_down, other_late_rows = lax.optimization_barrier((own_down, other_late_rows))
    other_down = swap(own_down)
    gate_grad, up_grad = call(
        kernel_joined,
        (shape(half, hidden), shape(half, hidden)),
        (
            rows_half,
            rows_half,
            shape(slots, 2 * hidden),
            shape(slots, 2 * hidden),
            shape(half, 2 * hidden),
        ),
        8,
        8 * slots * hidden * half,
        rows_in,
        late_rows,
        other_rows,
        other_late_rows,
        sides,
        other_sides,
    )
    picked, down_grad = call(
        kernel_final,
        (shape(entries, width), shape(hidden, width)),
        (
            shape(slots, entries),
            shape(slots, width),
            shape(entries, width),
            shape(2, hidden, half),
        ),
        9,
        2 * slots * entries * width,
        place,
        returned,
        own_down,
        other_down,
    )
    crowded = jnp.maximum(jnp.max(sent_late[slots:]), jnp.max(other_pre[slots:])) > 0.0
    return crowded, (sum_choices(picked, per_token), gate_grad[None], up_grad[None], down_grad[None])


def on_device(*arguments):
    if lax.axis_size("dp") != 2:
        return on_any(*arguments)
    crowded, results = on_pair(*arguments)
    return lax.while_loop(
        lambda state: state[0], lambda state: (False, on_any(*arguments)), (crowded, results)
    )[1]


def on_any(tokens, out_grad, expert_ids, gates, w_gate, w_up, w_down):
    experts = lax.axis_size("expert")
    width = tokens.shape[1]
    per_token = expert_ids.shape[1]
    hidden = w_gate.shape[2]
    depth = 3 * expert_ids.size // experts
    slots = experts * depth

    pair = lax.axis_size("dp") == 2
    first = lax.axis_index("dp") == 0

    def gather(x, axis):
        if not pair:
            return lax.all_gather(x, "dp", axis=axis, tiled=True)
        other = swap(x)
        return jnp.concatenate([jnp.where(first, x, other), jnp.where(first, other, x)], axis=axis)

    joined = gather(jnp.concatenate([w_gate[0], w_up[0]], axis=1), 0)
    down = gather(w_down[0], 1)
    place = place_matrix(expert_ids, experts, depth)

    def dispatch(table):
        sent = dot(place, table, (1, 0)).astype(BF16).reshape(experts, depth, width)
        return exchange(sent, "expert").reshape(slots, width)

    rows_in = dispatch(token_rows(tokens, per_token))
    grads_in = dispatch(scaled_rows(out_grad, gates))
    preact = dot(rows_in, joined, (1, 0))
    activated, sides = sides_of(
        preact[:, :hidden], preact[:, hidden:], dot(grads_in, down, (1, 1))
    )
    slot_grad = dot(sides, joined, (1, 1)).astype(BF16)
    returned = exchange(slot_grad.reshape(experts, depth, width), "expert").reshape(slots, width)
    down_part = dot(activated, grads_in, (0, 0)).astype(BF16)
    joined_part = dot(rows_in, sides, (0, 0)).astype(BF16)
    if pair:
        low, high = jnp.split(joined_part, 2, axis=0)
        down_grad = sum_parts(down_part, swap(down_part))
        joined_grad = sum_parts(jnp.where(first, low, high), swap(jnp.where(first, high, low)))
    else:
        down_grad = lax.psum(down_part, "dp")
        joined_grad = lax.psum_scatter(joined_part, "dp", scatter_dimension=0, tiled=True)
    input_grad = sum_choices(dot(place, returned, (0, 0)), per_token)
    return (
        input_grad,
        joined_grad[:, :hidden][None],
        joined_grad[:, hidden:][None],
        down_grad[None],
    )


def solution(mesh):
    rows = P(BOTH, None)
    in_specs = (
        rows,
        rows,
        rows,
        rows,
        P("expert", "dp", None),
        P("expert", "dp", None),
        P("expert", None, "dp"),
    )
    out_specs = (
        rows,
        P("expert", "dp", None),
        P("expert", "dp", None),
        P("expert", None, None),
    )
    return jax.shard_map(
        on_device, mesh=mesh, in_specs=in_specs, out_specs=out_specs, check_vma=False
    )
```
